256 devices in a mesh: layer: 8 (over z_lo, y), facet: 32 (over x, z_hi, core).
Axes of the slice: x: 4, y: 4, z: 8 (z_hi: 4, z_lo: 2; z = z_hi * 2 + z_lo), core: 2. Of those that a mesh axis runs over, the one named last changes fastest.
Arguments:
- slabs: bfloat16 [8, 2, 64, 98304], P('layer', None, None, 'facet'), may hold values from -6 to 6
- window: float32 [98304], P('facet'), may hold values from 0.5 to 1.5
- density: int32 [8, 64, 16384], P('layer', None, 'facet'), may hold values from 0 to 7
- offsets: int32 [32], replicated, may hold values from 0 to 98303
Outputs:
- image_out: float32 [2, 64, 98304], P(None, 'layer', 'facet')
The draws below stay inside these ranges and needn't reach their ends.
All inputs are finite; a program needn't handle non-finite values.
Results may differ from the reference program's by a relative error of at most 0.0052.
Values may be sent and summed in bfloat16 or wider, within the bound.
No kernel may reach another device: no remote copies, remote signals or barrier semaphores. Data moves between devices by JAX's collectives and lax.ppermute only.
A program may use at most 64 MiB of HBM per device.

```python
import math
import jax
import jax.numpy as jnp
from jax import lax

FACET = 3072
CONTRIB = 128
SUB = 512
COLS = 64
LAYERS = 8
FACETS = 32
IMAGE = 98304


def touch_ends(drawn, rng, smallest, largest):
    longest = drawn.shape.index(max(drawn.shape))
    spots = []
    for shift in (0, 1):
        where = [jax.random.randint(jax.random.fold_in(rng, axis), (), 0, length) for axis, length in enumerate(drawn.shape)]
        where[longest] = (where[longest] + shift) % drawn.shape[longest]
        spots.append(tuple(where))
    return drawn.at[spots[0]].set(smallest).at[spots[1]].set(largest)


def levels(stream_key, extent, shards, least, top_value):
    def one(dim, blocks):
        steps = jax.random.uniform(jax.random.fold_in(jax.random.fold_in(stream_key, 6), dim), (blocks,), jnp.float32, least / len(shards), top_value / len(shards))
        return jnp.repeat(jnp.exp(steps), extent[dim] // blocks).reshape((-1,) + (1,) * (len(extent) - dim - 1))

    gain = one(*shards[0])
    for cut in shards[1:]:
        gain = gain * one(*cut)
    return gain


def gaussian(own_key, shape, spread, most, shards=(), held_as=jnp.bfloat16):
    gain = levels(own_key, shape, shards, -0.22, 0.18) if shards else 1.0
    result = jax.random.normal(own_key, shape, jnp.float32) * spread * gain
    return jnp.minimum(jnp.maximum(result, -most), most).astype(held_as)


def setup_inputs(seed: int = 0) -> dict:
    streams_of = jax.random.split(jax.random.key(seed), 5)
    return {
        "slabs": gaussian(streams_of[0], (LAYERS, 2, COLS, IMAGE), 1.0, 6.0, ((0, 8), (3, 32))),
        "window": jnp.clip(0.5 + 1.0 * jax.random.uniform(streams_of[1], (IMAGE,), jnp.float32) ** levels(streams_of[1], (IMAGE,), ((0, 32),), -0.2, 0.2), 0.5, 1.5),
        "density": touch_ends(jax.random.randint(streams_of[2], (LAYERS, COLS, FACETS * SUB), 0, 8), jax.random.fold_in(streams_of[2], 1), 0, 7).astype(jnp.int32),
        "offsets": touch_ends(jax.random.randint(streams_of[3], (FACETS,), 0, IMAGE), jax.random.fold_in(streams_of[3], 1), 0, IMAGE - 1).astype(jnp.int32),
    }


two_pi = 2.0 * math.pi


def mulmod(left_term, right_term, modulus):
    upper_part = right_term // 256
    lower_part = right_term % 256
    return jnp.mod(jnp.mod(left_term * upper_part, modulus) * 256 + left_term * lower_part, modulus)


def encode_table(offset_block, x_start, facet_width, contrib_len, sample_step, image_width):
    frequencies = jnp.mod(offset_block[:, None] + sample_step * jnp.arange(contrib_len, dtype=jnp.int32)[None, :], image_width)
    places = x_start + jnp.arange(facet_width, dtype=jnp.int32)
    phase_turns = mulmod(frequencies[:, :, None], places[None, None, :], image_width)
    phase_angle = phase_turns.astype(jnp.float32) * (-two_pi / image_width)
    return jnp.stack([jnp.cos(phase_angle), jnp.sin(phase_angle)], 1).astype(jnp.bfloat16)


def embed_table(facet_count, facet_width, contrib_len, sub_len, image_width):
    sample_step = sub_len // contrib_len
    centres = jnp.arange(facet_count, dtype=jnp.int32) * facet_width + facet_width // 2
    sample_pos = jnp.arange(contrib_len, dtype=jnp.int32) * sample_step
    cell_ids = jnp.arange(sub_len, dtype=jnp.int32)
    spacing = cell_ids[None, :] - sample_pos[:, None]
    phase_turns = jnp.mod(spacing[None, :, :] * centres[:, None, None], image_width)
    phase_angle = phase_turns.astype(jnp.float32) * (-two_pi / image_width)
    scaled = spacing.astype(jnp.float32) / sample_step
    kernel = 1.0 / (1.0 + scaled * scaled)
    return jnp.stack([jnp.cos(phase_angle) * kernel, jnp.sin(phase_angle) * kernel], 1).astype(jnp.bfloat16)


def reference(slabs, window, density, offsets):
    sample_step = SUB // CONTRIB
    image_width = FACET * FACETS
    blocks = FACETS // 4
    windowed = (slabs.astype(jnp.float32) * window[None, None, None, :]).astype(jnp.bfloat16)
    block_ids = jnp.arange(blocks, dtype=jnp.int32)
    facet_ids = jnp.arange(FACETS, dtype=jnp.int32)

    def encode_facet(facet_id):
        facet_piece = lax.dynamic_slice_in_dim(windowed, facet_id * FACET, FACET, 3).astype(jnp.float32)

        def one_block(block_id):
            phase_table = encode_table(lax.dynamic_slice_in_dim(offsets, block_id * 4, 4, 0), facet_id * FACET, FACET, CONTRIB, sample_step, image_width).astype(jnp.float32)
            raw_prod = jnp.einsum("lpcx,bqjx->lpcbqj", facet_piece, phase_table)
            real_part = raw_prod[:, 0, :, :, 0] - raw_prod[:, 1, :, :, 1]
            imag_part = raw_prod[:, 0, :, :, 1] + raw_prod[:, 1, :, :, 0]
            return jnp.stack([real_part, imag_part], 1)

        pieces = lax.map(one_block, block_ids)
        pieces = jnp.transpose(pieces, (1, 0, 4, 2, 3, 5)).reshape(LAYERS, FACETS, 2, COLS, CONTRIB)
        return (pieces * FACET ** -0.5).astype(jnp.bfloat16)

    encoded = lax.map(encode_facet, facet_ids)
    embed_phase = embed_table(FACETS, FACET, CONTRIB, SUB, image_width).astype(jnp.float32)

    def subgrid_pass(sub_id):
        received = lax.dynamic_index_in_dim(encoded, sub_id, 2, keepdims=False).astype(jnp.float32)
        raw_prod = jnp.einsum("flpcj,fqju->lpcqu", received, embed_phase)
        real_part = raw_prod[:, 0, :, 0] - raw_prod[:, 1, :, 1]
        imag_part = raw_prod[:, 0, :, 1] + raw_prod[:, 1, :, 0]
        counts = lax.dynamic_slice_in_dim(density, sub_id * SUB, SUB, 2)
        weights = jnp.where(counts > 0, 1.0 / jnp.maximum(counts, 1).astype(jnp.float32), jnp.zeros(counts.shape, jnp.float32))
        gridded = (jnp.stack([real_part, imag_part], 1) * weights[:, None] * (2 * FACETS) ** -0.5).astype(jnp.bfloat16)
        raw_back = jnp.einsum("lpcu,fqju->lpcfqj", gridded.astype(jnp.float32), embed_phase)
        real_back = raw_back[:, 0, :, :, 0] + raw_back[:, 1, :, :, 1]
        imag_back = raw_back[:, 1, :, :, 0] - raw_back[:, 0, :, :, 1]
        return (jnp.stack([real_back, imag_back], 1) * 0.5).astype(jnp.bfloat16)

    returned = lax.map(subgrid_pass, facet_ids)

    def adjoint_facet(facet_id):
        row_block = lax.dynamic_index_in_dim(returned, facet_id, 4, keepdims=False)

        def one_block(running, block_id):
            phase_table = encode_table(lax.dynamic_slice_in_dim(offsets, block_id * 4, 4, 0), facet_id * FACET, FACET, CONTRIB, sample_step, image_width).astype(jnp.float32)
            part_rows = lax.dynamic_slice_in_dim(row_block, block_id * 4, 4, 0).astype(jnp.float32)
            raw_prod = jnp.einsum("blpcj,bqjx->lpcqx", part_rows, phase_table)
            real_part = raw_prod[:, 0, :, 0] + raw_prod[:, 1, :, 1]
            imag_part = raw_prod[:, 1, :, 0] - raw_prod[:, 0, :, 1]
            return running + jnp.stack([real_part, imag_part], 1), None

        running, unused = lax.scan(one_block, jnp.zeros((LAYERS, 2, COLS, FACET), jnp.float32), block_ids)
        taper_row = lax.dynamic_slice_in_dim(window, facet_id * FACET, FACET, 0)
        return jnp.sum(running * taper_row * (FACETS * CONTRIB) ** -0.5, axis=0)

    facet_out = lax.map(adjoint_facet, facet_ids)
    return jnp.transpose(facet_out, (1, 2, 0, 3)).reshape(2, COLS, FACETS * FACET)
```

```python
import math

import jax
import jax.numpy as jnp
import ml_dtypes
import numpy as np
from jax import lax
from jax.experimental import pallas as pl
from jax.experimental.pallas import tpu as pltpu
from jax.sharding import PartitionSpec as P

CONTRIB = 128
SUB = 512
LANES = 128
GROUP = 4

two_pi = 2.0 * math.pi
NT = (((1,), (1,)), ((), ()))
NN = (((1,), (0,)), ((), ()))


def mulmod(left_term, right_term, modulus):
    upper_part = right_term // 256
    lower_part = right_term % 256
    return jnp.mod(jnp.mod(left_term * upper_part, modulus) * 256 + left_term * lower_part, modulus)


def offset_phases(offsets, places, image_width):
    phase_turns = mulmod(offsets[:, None], places[None, :], image_width)
    phase_angle = phase_turns.astype(jnp.float32) * (two_pi / image_width)
    return jnp.cos(phase_angle), jnp.sin(phase_angle)


def step_table(facet_width, image_width, sample_step):
    j = np.arange(CONTRIB, dtype=np.int64)[:, None]
    cell = np.arange(facet_width, dtype=np.int64)[None, :] - facet_width // 2
    angle = np.mod(sample_step * j * cell, image_width) * (-2.0 * np.pi / image_width)
    return np.concatenate([np.cos(angle), np.sin(angle)], 0).astype(ml_dtypes.bfloat16)


def kernel_table(sample_step):
    spacing = np.arange(SUB)[None, :] - sample_step * np.arange(CONTRIB)[:, None]
    scaled = spacing / sample_step
    return (1.0 / (1.0 + scaled * scaled)).astype(ml_dtypes.bfloat16)


def centre_phases(facets):
    turns = np.mod(
        np.arange(SUB)[None, :] * (2 * np.arange(facets)[:, None] + 1), 2 * facets
    )
    angle = turns * (np.pi / facets)
    return np.cos(angle).astype(np.float32), np.sin(angle).astype(np.float32)


def fill_phases(hc_ref, hs_ref, lc_ref, ls_ref, pr_ref, pi_ref):
    lc, ls = lc_ref[...], ls_ref[...]
    for tile in range(pr_ref.shape[1] // LANES):
        hc = hc_ref[:, tile : tile + 1]
        hs = hs_ref[:, tile : tile + 1]
        span = slice(tile * LANES, (tile + 1) * LANES)
        pr_ref[:, span] = hc * lc - hs * ls
        pi_ref[:, span] = hs * lc + hc * ls


def encode_kernel(
    slab_ref, window_ref, hc_ref, hs_ref, lc_ref, ls_ref, table_ref, out_ref, w_ref, pr_ref, pi_ref
):
    columns = slab_ref.shape[0] // 2
    width = slab_ref.shape[1]
    step = pl.program_id(0)

    @pl.when(step == 0)
    def _():
        fill_phases(hc_ref, hs_ref, lc_ref, ls_ref, pr_ref, pi_ref)
        for tile in range(width // 256):
            span = slice(tile * 256, (tile + 1) * 256)
            windowed = slab_ref[:, span].astype(jnp.float32) * window_ref[:, span]
            w_ref[:, span] = windowed.astype(jnp.bfloat16).astype(jnp.float32)

    total = None
    for tile in range(width // 256):
        span = slice(tile * 256, (tile + 1) * 256)
        wr = w_ref[0:columns, span]
        wi = w_ref[columns : 2 * columns, span]
        rows = []
        for k in range(GROUP):
            pr = pr_ref[pl.ds(step * GROUP + k, 1), span]
            pi = pi_ref[pl.ds(step * GROUP + k, 1), span]
            rows.append((pr * wr + pi * wi).astype(jnp.bfloat16))
            rows.append((pr * wi - pi * wr).astype(jnp.bfloat16))
        part = lax.dot_general(
            jnp.concatenate(rows, 0), table_ref[:, span], NT, preferred_element_type=jnp.float32
        )
        total = part if total is None else total + part
    scale = width ** (-0.5)
    for k in range(GROUP):
        base = 2 * columns * k
        upper = total[base : base + columns]
        lower = total[base + columns : base + 2 * columns]
        out_ref[k, 0:columns, :] = (
            (upper[:, :CONTRIB] - lower[:, CONTRIB:]) * scale
        ).astype(jnp.bfloat16)
        out_ref[k, columns : 2 * columns, :] = (
            (upper[:, CONTRIB:] + lower[:, :CONTRIB]) * scale
        ).astype(jnp.bfloat16)


def grid_kernel(recv_ref, kernel_ref, cos_ref, sin_ref, counts_ref, out_ref, re_ref, im_ref):
    facets = recv_ref.shape[0]
    columns = recv_ref.shape[1] // 2
    re_ref[...] = jnp.zeros_like(re_ref)
    im_ref[...] = jnp.zeros_like(im_ref)

    def body(block, carry):
        re, im = None, None
        for k in range(4):
            f = block * 4 + k
            spread = lax.dot_general(
                recv_ref[f], kernel_ref[...], NN, preferred_element_type=jnp.float32
            )
            c = cos_ref[pl.ds(f, 1), :]
            s = sin_ref[pl.ds(f, 1), :]
            a, b = spread[:columns], spread[columns:]
            re_term = a * c + b * s
            im_term = b * c - a * s
            re = re_term if re is None else re + re_term
            im = im_term if im is None else im + im_term
        re_ref[...] += re
        im_ref[...] += im
        return carry

    lax.fori_loop(0, facets // 4, body, 0)
    counts = counts_ref[...]
    weights = jnp.where(
        counts > 0, 1.0 / jnp.maximum(counts, 1).astype(jnp.float32), 0.0
    ) * ((2 * facets) ** (-0.5))
    re = re_ref[...] * weights
    im = im_ref[...] * weights
    per = out_ref.shape[1] // 2
    for layer in range(out_ref.shape[0]):
        span = slice(layer * per, (layer + 1) * per)
        out_ref[layer] = jnp.concatenate([re[span], im[span]], 0).astype(jnp.bfloat16)


def back_kernel(recv_ref, kernel_ref, cos_ref, sin_ref, out_ref, rows_ref):
    layers = recv_ref.shape[0]
    facets = out_ref.shape[0]
    total = recv_ref[0].astype(jnp.float32)
    for layer in range(1, layers):
        total = total + recv_ref[layer].astype(jnp.float32)
    per = total.shape[0] // 2
    re, im = total[:per], total[per:]
    for f in range(facets):
        c = cos_ref[f : f + 1, :]
        s = sin_ref[f : f + 1, :]
        turned = jnp.concatenate([re * c - im * s, im * c + re * s], 0)
        rows_ref[f * 2 * per : (f + 1) * 2 * per, :] = turned.astype(jnp.bfloat16)
    back = lax.dot_general(
        rows_ref[...], kernel_ref[...], NT, preferred_element_type=jnp.float32
    )
    out_ref[...] = (back * 0.5).astype(jnp.bfloat16).reshape(out_ref.shape)


def decode_kernel(
    recv_ref, window_ref, hc_ref, hs_ref, lc_ref, ls_ref, table_ref, out_ref, pr_ref, pi_ref
):
    subgrids = recv_ref.shape[0]
    per = recv_ref.shape[1] // 2
    width = out_ref.shape[2]
    fill_phases(hc_ref, hs_ref, lc_ref, ls_ref, pr_ref, pi_ref)
    rows = recv_ref[...].astype(jnp.float32)
    re, im = rows[:, :per], rows[:, per:]
    left_re = jnp.concatenate([re, im], 2).reshape(subgrids * per, 2 * CONTRIB).astype(jnp.bfloat16)
    left_im = jnp.concatenate([im, -re], 2).reshape(subgrids * per, 2 * CONTRIB).astype(jnp.bfloat16)
    scale = (subgrids * CONTRIB) ** (-0.5)
    for tile in range(width // 256):
        span = slice(tile * 256, (tile + 1) * 256)
        table = table_ref[:, span]
        zr = lax.dot_general(left_re, table, NN, preferred_element_type=jnp.float32)
        zi = lax.dot_general(left_im, table, NN, preferred_element_type=jnp.float32)
        out_re, out_im = None, None
        for s in range(subgrids):
            a = zr[s * per : (s + 1) * per]
            b = zi[s * per : (s + 1) * per]
            pr = pr_ref[s : s + 1, span]
            pi = pi_ref[s : s + 1, span]
            re_term = pr * a - pi * b
            im_term = pr * b + pi * a
            out_re = re_term if out_re is None else out_re + re_term
            out_im = im_term if out_im is None else out_im + im_term
        taper = window_ref[:, span] * scale
        out_ref[0, :, span] = out_re * taper
        out_ref[1, :, span] = out_im * taper


def params(**more):
    return pltpu.CompilerParams(vmem_limit_bytes=48 * 2**20, **more)


def shards(slabs, window, density, offsets):
    layers = lax.axis_size("layer")
    facets = lax.axis_size("facet")
    position = lax.axis_index("facet")
    columns, width = slabs.shape[2], slabs.shape[3]
    per = columns // layers
    sample_step = SUB // CONTRIB
    image_width = width * facets
    tiles = width // LANES
    table = jnp.asarray(step_table(width, image_width, sample_step))
    spread = jnp.asarray(kernel_table(sample_step))
    cos_u, sin_u = (jnp.asarray(part) for part in centre_phases(facets))

    residues = jnp.mod(offsets, image_width)
    starts = position * width + LANES * jnp.arange(tiles, dtype=jnp.int32)
    hc, hs = offset_phases(residues, starts, image_width)
    lc, ls = offset_phases(residues, jnp.arange(LANES, dtype=jnp.int32), image_width)
    window_row = window.reshape(1, width)

    whole = pl.BlockSpec(memory_space=pltpu.VMEM)
    outgoing = pl.pallas_call(
        encode_kernel,
        grid=(facets // GROUP,),
        out_shape=jax.ShapeDtypeStruct((facets, 2 * columns, CONTRIB), jnp.bfloat16),
        in_specs=[whole] * 7,
        out_specs=pl.BlockSpec((GROUP, 2 * columns, CONTRIB), lambda g: (g, 0, 0)),
        scratch_shapes=[
            pltpu.VMEM((2 * columns, width), jnp.float32),
            pltpu.VMEM((facets, width), jnp.float32),
            pltpu.VMEM((facets, width), jnp.float32),
        ],
        compiler_params=params(),
        name="encode",
    )(slabs.reshape(2 * columns, width), window_row, hc, hs, lc, ls, table)

    received = lax.all_to_all(outgoing, "facet", split_axis=0, concat_axis=0, tiled=True)

    gridded = pl.pallas_call(
        grid_kernel,
        out_shape=jax.ShapeDtypeStruct((layers, 2 * per, SUB), jnp.bfloat16),
        in_specs=[whole] * 5,
        out_specs=whole,
        scratch_shapes=[pltpu.VMEM((columns, SUB), jnp.float32)] * 2,
        compiler_params=params(),
        name="subgrid",
    )(received, spread, cos_u, sin_u, density[0])

    by_layer = lax.all_to_all(gridded, "layer", split_axis=0, concat_axis=0, tiled=True)

    back_out = pl.pallas_call(
        back_kernel,
        out_shape=jax.ShapeDtypeStruct((facets, 2 * per, CONTRIB), jnp.bfloat16),
        in_specs=[whole] * 4,
        out_specs=whole,
        scratch_shapes=[pltpu.VMEM((facets * 2 * per, SUB), jnp.bfloat16)],
        compiler_params=params(),
        name="back",
    )(by_layer, spread, cos_u, sin_u)

    returned = lax.all_to_all(back_out, "facet", split_axis=0, concat_axis=0, tiled=True)

    return pl.pallas_call(
        decode_kernel,
        out_shape=jax.ShapeDtypeStruct((2, per, width), jnp.float32),
        in_specs=[whole] * 7,
        out_specs=whole,
        scratch_shapes=[pltpu.VMEM((facets, width), jnp.float32)] * 2,
        compiler_params=params(),
        name="decode",
    )(returned, window_row, hc, hs, lc, ls, table)


def solution(mesh):
    placed = (P("layer", None, None, "facet"), P("facet"), P("layer", None, "facet"), P())
    return jax.shard_map(
        shards, mesh=mesh, in_specs=placed, out_specs=P(None, "layer", "facet"), check_vma=False
    )
```

```python
import math

import jax
import jax.numpy as jnp
import ml_dtypes
import numpy as np
from jax import lax
from jax.experimental import pallas as pl
from jax.experimental.pallas import tpu as pltpu
from jax.sharding import PartitionSpec as P

CONTRIB = 128
SUB = 512
LANES = 128
GROUP = 8

two_pi = 2.0 * math.pi
NT = (((1,), (1,)), ((), ()))
NN = (((1,), (0,)), ((), ()))


def step_table(facet_width, image_width, sample_step):
    j = np.arange(CONTRIB, dtype=np.int64)[:, None]
    cell = np.arange(facet_width, dtype=np.int64)[None, :] - facet_width // 2
    angle = np.mod(sample_step * j * cell, image_width) * (-2.0 * np.pi / image_width)
    return np.concatenate([np.cos(angle), np.sin(angle)], 0).astype(ml_dtypes.bfloat16)


def kernel_table(sample_step):
    spacing = np.arange(SUB)[None, :] - sample_step * np.arange(CONTRIB)[:, None]
    scaled = spacing / sample_step
    return (1.0 / (1.0 + scaled * scaled)).astype(ml_dtypes.bfloat16)


def centre_phases(facets):
    turns = np.mod(
        np.arange(SUB)[None, :] * (2 * np.arange(facets)[:, None] + 1), 2 * facets
    )
    angle = turns * (np.pi / facets)
    return np.cos(angle).astype(np.float32), np.sin(angle).astype(np.float32)


def offset_tables(offsets_ref, position, tiles, image_width):
    subgrids = offsets_ref.shape[1]
    down = lax.broadcasted_iota(jnp.int32, (subgrids, subgrids), 0)
    across = lax.broadcasted_iota(jnp.int32, (subgrids, subgrids), 1)
    column = jnp.sum(jnp.where(down == across, offsets_ref[...], 0), axis=1, keepdims=True)
    lane = lax.broadcasted_iota(jnp.int32, (subgrids, LANES), 1)

    def parts(product, modulus):
        whole = jnp.floor(product.astype(jnp.float32) * (1.0 / modulus)).astype(jnp.int32)
        angle = (product - whole * modulus).astype(jnp.float32) * (two_pi / modulus)
        return jnp.cos(angle), jnp.sin(angle)

    high = parts(column * (position * tiles + lane), image_width // LANES)
    low = parts(column * lane, image_width)
    return high + low


def phases(tables, width):
    hc, hs, lc, ls = tables
    for tile in range(width // LANES):
        c = hc[:, tile : tile + 1]
        s = hs[:, tile : tile + 1]
        span = slice(tile * LANES, (tile + 1) * LANES)
        yield span, c * lc - s * ls, s * lc + c * ls


def encode_kernel(
    slab_hbm, window_hbm, offsets_ref, table_hbm, out_ref, tables_ref,
    slab_ref, window_ref, table_ref, w_ref, p_ref, sems,
):
    columns = slab_ref.shape[0] // 2
    width = slab_ref.shape[1]
    step = pl.program_id(0)

    @pl.when(step == 0)
    def _():
        copies = [
            pltpu.make_async_copy(slab_hbm, slab_ref, sems.at[0]),
            pltpu.make_async_copy(window_hbm, window_ref, sems.at[1]),
            pltpu.make_async_copy(table_hbm, table_ref, sems.at[2]),
        ]
        for copy in copies:
            copy.start()
        tables = offset_tables(
            offsets_ref, lax.axis_index("facet"), width // LANES, width * offsets_ref.shape[1]
        )
        for k in range(4):
            tables_ref[k] = tables[k]
        for span, pr, pi in phases(tables, width):
            p_ref[0, :, span] = pr
            p_ref[1, :, span] = pr - pi
            p_ref[2, :, span] = pr + pi
        copies[0].wait()
        copies[1].wait()
        for tile in range(width // 256):
            span = slice(tile * 256, (tile + 1) * 256)
            windowed = slab_ref[:, span].astype(jnp.float32) * window_ref[:, span]
            windowed = windowed.astype(jnp.bfloat16).astype(jnp.float32)
            w_ref[0 : 2 * columns, span] = windowed
            w_ref[2 * columns :, span] = windowed[:columns] + windowed[columns:]
        copies[2].wait()

    total = None
    for tile in range(width // 256):
        span = slice(tile * 256, (tile + 1) * 256)
        wr = w_ref[0:columns, span]
        wi = w_ref[columns : 2 * columns, span]
        both = w_ref[2 * columns :, span]
        rows = []
        for k in range(GROUP):
            real, less, more = (p_ref[n, pl.ds(step * GROUP + k, 1), span] for n in range(3))
            shared = real * both
            rows.append((shared - less * wi).astype(jnp.bfloat16))
            rows.append((shared - more * wr).astype(jnp.bfloat16))
        part = lax.dot_general(
            jnp.concatenate(rows, 0), table_ref[span, :], NN, preferred_element_type=jnp.float32
        )
        total = part if total is None else total + part
    scale = width ** (-0.5)
    for k in range(GROUP):
        base = 2 * columns * k
        upper = total[base : base + columns]
        lower = total[base + columns : base + 2 * columns]
        out_ref[k, 0:columns, :] = (
            (upper[:, :CONTRIB] - lower[:, CONTRIB:]) * scale
        ).astype(jnp.bfloat16)
        out_ref[k, columns : 2 * columns, :] = (
            (upper[:, CONTRIB:] + lower[:, :CONTRIB]) * scale
        ).astype(jnp.bfloat16)


def grid_kernel(recv_ref, kernel_ref, cos_ref, sin_ref, counts_ref, out_ref, re_ref, im_ref):
    facets = recv_ref.shape[0]
    columns = recv_ref.shape[1] // 2
    re_ref[...] = jnp.zeros_like(re_ref)
    im_ref[...] = jnp.zeros_like(im_ref)

    def body(block, carry):
        re, im = None, None
        for k in range(4):
            f = block * 4 + k
            spread = lax.dot_general(
                recv_ref[f], kernel_ref[...], NN, preferred_element_type=jnp.float32
            )
            c = cos_ref[pl.ds(f, 1), :]
            s = sin_ref[pl.ds(f, 1), :]
            a, b = spread[:columns], spread[columns:]
            re_term = a * c + b * s
            im_term = b * c - a * s
            re = re_term if re is None else re + re_term
            im = im_term if im is None else im + im_term
        re_ref[...] += re
        im_ref[...] += im
        return carry

    lax.fori_loop(0, facets // 4, body, 0)
    counts = counts_ref[...]
    weights = jnp.where(
        counts > 0, 1.0 / jnp.maximum(counts, 1).astype(jnp.float32), 0.0
    ) * ((2 * facets) ** (-0.5))
    re = re_ref[...] * weights
    im = im_ref[...] * weights
    per = out_ref.shape[1] // 2
    for layer in range(out_ref.shape[0]):
        span = slice(layer * per, (layer + 1) * per)
        out_ref[layer] = jnp.concatenate([re[span], im[span]], 0).astype(jnp.bfloat16)


def back_kernel(recv_ref, kernel_ref, cos_ref, sin_ref, out_ref, rows_ref):
    layers = recv_ref.shape[0]
    facets = out_ref.shape[0]
    total = recv_ref[0].astype(jnp.float32)
    for layer in range(1, layers):
        total = total + recv_ref[layer].astype(jnp.float32)
    per = total.shape[0] // 2
    re, im = total[:per], total[per:]
    for f in range(facets):
        c = cos_ref[f : f + 1, :]
        s = sin_ref[f : f + 1, :]
        turned = jnp.concatenate([re * c - im * s, im * c + re * s], 0)
        rows_ref[f * 2 * per : (f + 1) * 2 * per, :] = turned.astype(jnp.bfloat16)
    back = lax.dot_general(
        rows_ref[...], kernel_ref[...], NT, preferred_element_type=jnp.float32
    )
    out_ref[...] = (back * 0.5).astype(jnp.bfloat16).reshape(out_ref.shape)


def decode_kernel(
    recv_ref, window_ref, tables_ref, table_ref, out_ref, pr_ref, pi_ref
):
    subgrids = recv_ref.shape[0]
    per = recv_ref.shape[1] // 2
    width = out_ref.shape[2]
    for span, pr, pi in phases([tables_ref[k] for k in range(4)], width):
        pr_ref[:, span] = pr
        pi_ref[:, span] = pi
    rows = recv_ref[...].astype(jnp.float32)
    re, im = rows[:, :per], rows[:, per:]
    left_re = jnp.concatenate([re, im], 2).reshape(subgrids * per, 2 * CONTRIB).astype(jnp.bfloat16)
    left_im = jnp.concatenate([im, -re], 2).reshape(subgrids * per, 2 * CONTRIB).astype(jnp.bfloat16)
    scale = (subgrids * CONTRIB) ** (-0.5)
    for tile in range(width // 256):
        span = slice(tile * 256, (tile + 1) * 256)
        table = table_ref[:, span]
        zr = lax.dot_general(left_re, table, NN, preferred_element_type=jnp.float32)
        zi = lax.dot_general(left_im, table, NN, preferred_element_type=jnp.float32)
        out_re, out_im = None, None
        for s in range(subgrids):
            a = zr[s * per : (s + 1) * per]
            b = zi[s * per : (s + 1) * per]
            pr = pr_ref[s : s + 1, span]
            pi = pi_ref[s : s + 1, span]
            re_term = pr * a - pi * b
            im_term = pr * b + pi * a
            out_re = re_term if out_re is None else out_re + re_term
            out_im = im_term if out_im is None else out_im + im_term
        taper = window_ref[:, span] * scale
        out_ref[0, :, span] = out_re * taper
        out_ref[1, :, span] = out_im * taper


def params(mebibytes):
    return pltpu.CompilerParams(vmem_limit_bytes=mebibytes * 2**20)


def shards(slabs, window, density, offsets):
    layers = lax.axis_size("layer")
    facets = lax.axis_size("facet")
    columns, width = slabs.shape[2], slabs.shape[3]
    per = columns // layers
    sample_step = SUB // CONTRIB
    image_width = width * facets
    steps = step_table(width, image_width, sample_step)
    table, table_down = jnp.asarray(steps), jnp.asarray(np.ascontiguousarray(steps.T))
    spread = jnp.asarray(kernel_table(sample_step))
    cos_u, sin_u = (jnp.asarray(part) for part in centre_phases(facets))

    window_row = window.reshape(1, width)

    whole = pl.BlockSpec(memory_space=pltpu.VMEM)
    anywhere = pl.BlockSpec(memory_space=pl.ANY)
    outgoing, tables = pl.pallas_call(
        encode_kernel,
        grid=(facets // GROUP,),
        out_shape=(
            jax.ShapeDtypeStruct((facets, 2 * columns, CONTRIB), jnp.bfloat16),
            jax.ShapeDtypeStruct((4, facets, LANES), jnp.float32),
        ),
        in_specs=[anywhere, anywhere, whole, anywhere],
        out_specs=(
            pl.BlockSpec((GROUP, 2 * columns, CONTRIB), lambda g: (g, 0, 0)),
            pl.BlockSpec((4, facets, LANES), lambda g: (0, 0, 0)),
        ),
        scratch_shapes=[
            pltpu.VMEM((2 * columns, width), jnp.bfloat16),
            pltpu.VMEM((1, width), jnp.float32),
            pltpu.VMEM((width, 2 * CONTRIB), jnp.bfloat16),
            pltpu.VMEM((3 * columns, width), jnp.float32),
            pltpu.VMEM((3, facets, width), jnp.float32),
            pltpu.SemaphoreType.DMA((3,)),
        ],
        compiler_params=params(60),
        name="encode",
    )(slabs.reshape(2 * columns, width), window_row, offsets.reshape(1, facets), table_down)

    received = lax.all_to_all(outgoing, "facet", split_axis=0, concat_axis=0, tiled=True)

    gridded = pl.pallas_call(
        grid_kernel,
        out_shape=jax.ShapeDtypeStruct((layers, 2 * per, SUB), jnp.bfloat16),
        in_specs=[whole] * 5,
        out_specs=whole,
        scratch_shapes=[pltpu.VMEM((columns, SUB), jnp.float32)] * 2,
        compiler_params=params(48),
        name="subgrid",
    )(received, spread, cos_u, sin_u, density[0])

    by_layer = lax.all_to_all(gridded, "layer", split_axis=0, concat_axis=0, tiled=True)

    back_out = pl.pallas_call(
        back_kernel,
        out_shape=jax.ShapeDtypeStruct((facets, 2 * per, CONTRIB), jnp.bfloat16),
        in_specs=[whole] * 4,
        out_specs=whole,
        scratch_shapes=[pltpu.VMEM((facets * 2 * per, SUB), jnp.bfloat16)],
        compiler_params=params(48),
        name="back",
    )(by_layer, spread, cos_u, sin_u)

    returned = lax.all_to_all(back_out, "facet", split_axis=0, concat_axis=0, tiled=True)

    return pl.pallas_call(
        decode_kernel,
        out_shape=jax.ShapeDtypeStruct((2, per, width), jnp.float32),
        in_specs=[whole] * 4,
        out_specs=whole,
        scratch_shapes=[pltpu.VMEM((facets, width), jnp.float32)] * 2,
        compiler_params=params(48),
        name="decode",
    )(returned, window_row, tables, table)


def solution(mesh):
    placed = (P("layer", None, None, "facet"), P("facet"), P("layer", None, "facet"), P())
    return jax.shard_map(
        shards, mesh=mesh, in_specs=placed, out_specs=P(None, "layer", "facet"), check_vma=False
    )
```

```python
import math

import jax
import jax.numpy as jnp
import ml_dtypes
import numpy as np
from jax import lax
from jax.experimental import pallas as pl
from jax.experimental.pallas import tpu as pltpu
from jax.sharding import PartitionSpec as P

CONTRIB = 128
SUB = 512
LANES = 128
FINE = 4
STEP = 256

two_pi = 2.0 * math.pi
NT = (((1,), (1,)), ((), ()))
NN = (((1,), (0,)), ((), ()))


def step_table(facet_width, image_width, sample_step):
    j = np.arange(CONTRIB, dtype=np.int64)[:, None]
    cell = np.arange(facet_width, dtype=np.int64)[None, :] - facet_width // 2
    angle = np.mod(sample_step * j * cell, image_width) * (-2.0 * np.pi / image_width)
    return np.concatenate([np.cos(angle), np.sin(angle)], 0).astype(ml_dtypes.bfloat16)


def fold_tables(facet_width, image_width, sample_step):
    k = np.arange(facet_width // 2, dtype=np.int64)[None, :]
    j1 = np.arange(CONTRIB // FINE, dtype=np.int64)[:, None]
    j2 = np.arange(FINE, dtype=np.int64)[:, None]

    def parts(turns):
        angle = np.mod(turns, image_width) * (2.0 * np.pi / image_width)
        return np.stack([np.cos(angle), np.sin(angle)]).astype(np.float32)

    half_step = sample_step * FINE // 2
    coarse = parts(half_step * j1 * (2 * k + 1))
    fine = np.stack([parts(sample_step * j2 * k), parts(-sample_step * j2 * (k + 1))])
    fine = fine.transpose(2, 0, 1, 3).reshape(4 * FINE, facet_width // 2)
    turn = np.broadcast_to(parts(half_step * j1), (2, CONTRIB // FINE, LANES))
    flip = np.eye(STEP)[::-1].astype(ml_dtypes.bfloat16)
    return coarse, np.ascontiguousarray(fine), np.ascontiguousarray(turn), np.ascontiguousarray(flip)


def kernel_table(sample_step):
    spacing = np.arange(SUB)[None, :] - sample_step * np.arange(CONTRIB)[:, None]
    scaled = spacing / sample_step
    return (1.0 / (1.0 + scaled * scaled)).astype(ml_dtypes.bfloat16)


def centre_phases(facets):
    turns = np.mod(
        np.arange(SUB)[None, :] * (2 * np.arange(facets)[:, None] + 1), 2 * facets
    )
    angle = turns * (np.pi / facets)
    return np.cos(angle).astype(np.float32), np.sin(angle).astype(np.float32)


def offset_tables(offsets_ref, position, width):
    subgrids = offsets_ref.shape[1]
    image_width = width * subgrids
    down = lax.broadcasted_iota(jnp.int32, (subgrids, subgrids), 0)
    across = lax.broadcasted_iota(jnp.int32, (subgrids, subgrids), 1)
    column = jnp.sum(jnp.where(down == across, offsets_ref[...], 0), axis=1, keepdims=True)
    lane = lax.broadcasted_iota(jnp.int32, (subgrids, LANES), 1)

    def parts(product, modulus):
        whole = jnp.floor(product.astype(jnp.float32) * (1.0 / modulus)).astype(jnp.int32)
        angle = (product - whole * modulus).astype(jnp.float32) * (two_pi / modulus)
        return jnp.cos(angle), jnp.sin(angle)

    facet_turns = jnp.bitwise_and(column * position, subgrids - 1)
    return {
        "start": parts(column * (position * (width // LANES) + lane), image_width // LANES),
        "cell": parts(column * lane, image_width),
        "tile": parts(column * lane, image_width // LANES),
        "inner": parts(column * (2 * lane + 1), 2 * image_width),
        "middle": parts(
            column * (width - 1) + 2 * width * facet_turns + 0 * lane, 2 * image_width
        ),
    }


def encode_kernel(
    slab_hbm, window_hbm, offsets_ref, coarse_hbm, fine_hbm, turn_hbm, flip_hbm, out_ref, tables_ref,
    slab_ref, window_ref, coarse_ref, fine_ref, turn_ref, flip_ref,
    phase_ref, cos_ref, sin_ref, even_ref, odd_ref, total_ref, sems,
):
    columns = slab_ref.shape[0] // 2
    width = slab_ref.shape[1]
    half = width // 2
    subgrids = offsets_ref.shape[1]
    rows = CONTRIB // FINE
    pairs = (
        (slab_hbm, slab_ref), (window_hbm, window_ref), (coarse_hbm, coarse_ref),
        (fine_hbm, fine_ref), (turn_hbm, turn_ref), (flip_hbm, flip_ref),
    )
    copies = [pltpu.make_async_copy(a, b, sems.at[n]) for n, (a, b) in enumerate(pairs)]
    for copy in copies:
        copy.start()
    turns = offset_tables(offsets_ref, lax.axis_index("facet"), width)
    for n in range(2):
        tables_ref[n] = turns["start"][n]
        tables_ref[2 + n] = turns["cell"][n]
    high, low, centre = turns["tile"], turns["inner"], turns["middle"]
    for tile in range(half // LANES):
        c, s = high[0][:, tile : tile + 1], high[1][:, tile : tile + 1]
        span = slice(tile * LANES, (tile + 1) * LANES)
        phase_ref[0, :, span] = c * low[0] - s * low[1]
        phase_ref[1, :, span] = s * low[0] + c * low[1]
    for copy in copies:
        copy.wait()

    def windowed(span):
        product = slab_ref[:, span].astype(jnp.float32) * window_ref[:, span]
        return product.astype(jnp.bfloat16)

    for tile in range(half // STEP):
        span = slice(tile * STEP, (tile + 1) * STEP)
        plus = windowed(slice(half + tile * STEP, half + (tile + 1) * STEP)).astype(jnp.float32)
        minus = lax.dot_general(
            windowed(slice(half - (tile + 1) * STEP, half - tile * STEP)), flip_ref[...], NN,
            preferred_element_type=jnp.float32,
        )
        for fine in range(FINE):
            sides = []
            for n, side in enumerate((plus, minus)):
                re, im = side[:columns], side[columns:]
                if fine > 0:
                    row = (2 * fine + n) * 2
                    c, s = fine_ref[row : row + 1, span], fine_ref[row + 1 : row + 2, span]
                    re, im = re * c + im * s, im * c - re * s
                sides.append((re, im))
            (re_p, im_p), (re_m, im_m) = sides
            base = 2 * columns * fine
            even_ref[base : base + columns] = (re_p + re_m).astype(jnp.bfloat16)
            even_ref[base + columns : base + 2 * columns] = (im_p + im_m).astype(jnp.bfloat16)
            odd_ref[base : base + columns] = (im_p - im_m).astype(jnp.bfloat16)
            odd_ref[base + columns : base + 2 * columns] = (re_m - re_p).astype(jnp.bfloat16)
        cj, sj = coarse_ref[0, :, span], coarse_ref[1, :, span]
        for s in range(subgrids):
            co, so = phase_ref[0, s : s + 1, span], phase_ref[1, s : s + 1, span]
            cos_ref[s * rows : (s + 1) * rows] = (co * cj - so * sj).astype(jnp.bfloat16)
            sin_ref[s * rows : (s + 1) * rows] = (so * cj + co * sj).astype(jnp.bfloat16)
        part = lax.dot_general(
            cos_ref[...], even_ref[...], NT, preferred_element_type=jnp.float32
        ) + lax.dot_general(sin_ref[...], odd_ref[...], NT, preferred_element_type=jnp.float32)
        if tile == 0:
            total_ref[...] = part
        else:
            total_ref[...] += part

    cj, sj = turn_ref[0], turn_ref[1]
    scale = width ** (-0.5)
    sign = jnp.where(
        lax.broadcasted_iota(jnp.int32, (1, 2 * columns), 1) < columns, scale, -scale
    )
    for s in range(subgrids):
        co, so = centre[0][s : s + 1], centre[1][s : s + 1]
        c = (co * cj + so * sj) * scale
        d = (so * cj - co * sj) * sign
        blocks = []
        for fine in range(FINE):
            block = total_ref[s * rows : (s + 1) * rows, fine * LANES : (fine + 1) * LANES]
            blocks.append(block * c + pltpu.roll(block, columns, 1) * d)
        out_ref[s] = jnp.concatenate(blocks, 0).T.astype(jnp.bfloat16)


def grid_kernel(recv_ref, kernel_ref, cos_ref, sin_ref, counts_ref, out_ref, re_ref, im_ref):
    facets = recv_ref.shape[0]
    columns = recv_ref.shape[1] // 2
    re_ref[...] = jnp.zeros_like(re_ref)
    im_ref[...] = jnp.zeros_like(im_ref)

    def body(block, carry):
        re, im = None, None
        for k in range(4):
            f = block * 4 + k
            spread = lax.dot_general(
                recv_ref[f], kernel_ref[...], NN, preferred_element_type=jnp.float32
            )
            c = cos_ref[pl.ds(f, 1), :]
            s = sin_ref[pl.ds(f, 1), :]
            a, b = spread[:columns], spread[columns:]
            re_term = a * c + b * s
            im_term = b * c - a * s
            re = re_term if re is None else re + re_term
            im = im_term if im is None else im + im_term
        re_ref[...] += re
        im_ref[...] += im
        return carry

    lax.fori_loop(0, facets // 4, body, 0)
    counts = counts_ref[...]
    weights = jnp.where(
        counts > 0, 1.0 / jnp.maximum(counts, 1).astype(jnp.float32), 0.0
    ) * ((2 * facets) ** (-0.5))
    re = re_ref[...] * weights
    im = im_ref[...] * weights
    per = out_ref.shape[1] // 2
    for layer in range(out_ref.shape[0]):
        span = slice(layer * per, (layer + 1) * per)
        out_ref[layer] = jnp.concatenate([re[span], im[span]], 0).astype(jnp.bfloat16)


def back_kernel(recv_ref, kernel_ref, cos_ref, sin_ref, out_ref, rows_ref):
    layers = recv_ref.shape[0]
    facets = out_ref.shape[0]
    total = recv_ref[0].astype(jnp.float32)
    for layer in range(1, layers):
        total = total + recv_ref[layer].astype(jnp.float32)
    per = total.shape[0] // 2
    re, im = total[:per], total[per:]
    for f in range(facets):
        c = cos_ref[f : f + 1, :]
        s = sin_ref[f : f + 1, :]
        turned = jnp.concatenate([re * c - im * s, im * c + re * s], 0)
        rows_ref[f * 2 * per : (f + 1) * 2 * per, :] = turned.astype(jnp.bfloat16)
    back = lax.dot_general(
        rows_ref[...], kernel_ref[...], NT, preferred_element_type=jnp.float32
    )
    out_ref[...] = (back * 0.5).astype(jnp.bfloat16).reshape(out_ref.shape)


def decode_kernel(
    recv_ref, window_ref, tables_ref, table_ref, out_ref, pr_ref, pi_ref
):
    subgrids = recv_ref.shape[0]
    per = recv_ref.shape[1] // 2
    width = out_ref.shape[2]
    for tile in range(width // LANES):
        c, s = tables_ref[0, :, tile : tile + 1], tables_ref[1, :, tile : tile + 1]
        span = slice(tile * LANES, (tile + 1) * LANES)
        pr_ref[:, span] = c * tables_ref[2] - s * tables_ref[3]
        pi_ref[:, span] = s * tables_ref[2] + c * tables_ref[3]
    rows = recv_ref[...].astype(jnp.float32)
    re, im = rows[:, :per], rows[:, per:]
    left_re = jnp.concatenate([re, im], 2).reshape(subgrids * per, 2 * CONTRIB).astype(jnp.bfloat16)
    left_im = jnp.concatenate([im, -re], 2).reshape(subgrids * per, 2 * CONTRIB).astype(jnp.bfloat16)
    scale = (subgrids * CONTRIB) ** (-0.5)
    for tile in range(width // 256):
        span = slice(tile * 256, (tile + 1) * 256)
        table = table_ref[:, span]
        zr = lax.dot_general(left_re, table, NN, preferred_element_type=jnp.float32)
        zi = lax.dot_general(left_im, table, NN, preferred_element_type=jnp.float32)
        out_re, out_im = None, None
        for s in range(subgrids):
            a = zr[s * per : (s + 1) * per]
            b = zi[s * per : (s + 1) * per]
            pr = pr_ref[s : s + 1, span]
            pi = pi_ref[s : s + 1, span]
            re_term = pr * a - pi * b
            im_term = pr * b + pi * a
            out_re = re_term if out_re is None else out_re + re_term
            out_im = im_term if out_im is None else out_im + im_term
        taper = window_ref[:, span] * scale
        out_ref[0, :, span] = out_re * taper
        out_ref[1, :, span] = out_im * taper


def params(mebibytes):
    return pltpu.CompilerParams(vmem_limit_bytes=mebibytes * 2**20)


def shards(slabs, window, density, offsets):
    layers = lax.axis_size("layer")
    facets = lax.axis_size("facet")
    columns, width = slabs.shape[2], slabs.shape[3]
    per = columns // layers
    sample_step = SUB // CONTRIB
    image_width = width * facets
    table = jnp.asarray(step_table(width, image_width, sample_step))
    folds = [jnp.asarray(part) for part in fold_tables(width, image_width, sample_step)]
    spreading = kernel_table(sample_step)
    spread = jnp.asarray(spreading)
    order = np.arange(CONTRIB).reshape(CONTRIB // FINE, FINE).T.reshape(-1)
    spread_in = jnp.asarray(np.ascontiguousarray(spreading[order]))
    cos_u, sin_u = (jnp.asarray(part) for part in centre_phases(facets))

    window_row = window.reshape(1, width)

    whole = pl.BlockSpec(memory_space=pltpu.VMEM)
    anywhere = pl.BlockSpec(memory_space=pl.ANY)
    rows = facets * CONTRIB // FINE
    wide = 2 * columns * FINE
    half = width // 2
    outgoing, tables = pl.pallas_call(
        encode_kernel,
        out_shape=(
            jax.ShapeDtypeStruct((facets, 2 * columns, CONTRIB), jnp.bfloat16),
            jax.ShapeDtypeStruct((4, facets, LANES), jnp.float32),
        ),
        in_specs=[anywhere, anywhere, whole] + [anywhere] * 4,
        out_specs=(whole, whole),
        scratch_shapes=[
            pltpu.VMEM((2 * columns, width), jnp.bfloat16),
            pltpu.VMEM((1, width), jnp.float32),
            pltpu.VMEM((2, CONTRIB // FINE, half), jnp.float32),
            pltpu.VMEM((4 * FINE, half), jnp.float32),
            pltpu.VMEM((2, CONTRIB // FINE, LANES), jnp.float32),
            pltpu.VMEM((STEP, STEP), jnp.bfloat16),
            pltpu.VMEM((2, facets, half), jnp.float32),
            pltpu.VMEM((rows, STEP), jnp.bfloat16),
            pltpu.VMEM((rows, STEP), jnp.bfloat16),
            pltpu.VMEM((wide, STEP), jnp.bfloat16),
            pltpu.VMEM((wide, STEP), jnp.bfloat16),
            pltpu.VMEM((rows, wide), jnp.float32),
            pltpu.SemaphoreType.DMA((6,)),
        ],
        compiler_params=params(60),
        name="encode",
    )(slabs.reshape(2 * columns, width), window_row, offsets.reshape(1, facets), *folds)

    received = lax.all_to_all(outgoing, "facet", split_axis=0, concat_axis=0, tiled=True)

    gridded = pl.pallas_call(
        grid_kernel,
        out_shape=jax.ShapeDtypeStruct((layers, 2 * per, SUB), jnp.bfloat16),
        in_specs=[whole] * 5,
        out_specs=whole,
        scratch_shapes=[pltpu.VMEM((columns, SUB), jnp.float32)] * 2,
        compiler_params=params(48),
        name="subgrid",
    )(received, spread_in, cos_u, sin_u, density[0])

    by_layer = lax.all_to_all(gridded, "layer", split_axis=0, concat_axis=0, tiled=True)

    back_out = pl.pallas_call(
        back_kernel,
        out_shape=jax.ShapeDtypeStruct((facets, 2 * per, CONTRIB), jnp.bfloat16),
        in_specs=[whole] * 4,
        out_specs=whole,
        scratch_shapes=[pltpu.VMEM((facets * 2 * per, SUB), jnp.bfloat16)],
        compiler_params=params(48),
        name="back",
    )(by_layer, spread, cos_u, sin_u)

    returned = lax.all_to_all(back_out, "facet", split_axis=0, concat_axis=0, tiled=True)

    return pl.pallas_call(
        decode_kernel,
        out_shape=jax.ShapeDtypeStruct((2, per, width), jnp.float32),
        in_specs=[whole] * 4,
        out_specs=whole,
        scratch_shapes=[pltpu.VMEM((facets, width), jnp.float32)] * 2,
        compiler_params=params(48),
        name="decode",
    )(returned, window_row, tables, table)


def solution(mesh):
    placed = (P("layer", None, None, "facet"), P("facet"), P("layer", None, "facet"), P())
    return jax.shard_map(
        shards, mesh=mesh, in_specs=placed, out_specs=P(None, "layer", "facet"), check_vma=False
    )
```

```python
import math

import jax
import jax.numpy as jnp
import ml_dtypes
import numpy as np
from jax import lax
from jax.experimental import pallas as pl
from jax.experimental.pallas import tpu as pltpu
from jax.sharding import PartitionSpec as P

CONTRIB = 128
SUB = 512
LANES = 128
FINE = 4
STEP = 256
BLOCKS = 2

two_pi = 2.0 * math.pi
NT = (((1,), (1,)), ((), ()))
NN = (((1,), (0,)), ((), ()))


def step_table(facet_width, image_width, sample_step):
    j = np.arange(CONTRIB, dtype=np.int64)[:, None]
    cell = np.arange(facet_width, dtype=np.int64)[None, :] - facet_width // 2
    angle = np.mod(sample_step * j * cell, image_width) * (-2.0 * np.pi / image_width)
    return np.concatenate([np.cos(angle), np.sin(angle)], 0).astype(ml_dtypes.bfloat16)


def fold_tables(facet_width, image_width, sample_step):
    k = np.arange(facet_width // 2, dtype=np.int64)[None, :]
    j1 = np.arange(CONTRIB // FINE, dtype=np.int64)[:, None]
    j2 = np.arange(FINE, dtype=np.int64)[:, None]

    def parts(turns):
        angle = np.mod(turns, image_width) * (2.0 * np.pi / image_width)
        return np.stack([np.cos(angle), np.sin(angle)]).astype(np.float32)

    half_step = sample_step * FINE // 2
    coarse = parts(half_step * j1 * (2 * k + 1))
    fine = np.stack([parts(sample_step * j2 * k), parts(-sample_step * j2 * (k + 1))])
    fine = fine.transpose(2, 0, 1, 3).reshape(4 * FINE, facet_width // 2)
    turn = np.broadcast_to(parts(half_step * j1), (2, CONTRIB // FINE, LANES))
    flip = np.eye(STEP)[::-1].astype(ml_dtypes.bfloat16)
    return coarse, np.ascontiguousarray(fine), np.ascontiguousarray(turn), np.ascontiguousarray(flip)


def kernel_table(sample_step):
    spacing = np.arange(SUB)[None, :] - sample_step * np.arange(CONTRIB)[:, None]
    scaled = spacing / sample_step
    return (1.0 / (1.0 + scaled * scaled)).astype(ml_dtypes.bfloat16)


def centre_phases(facets):
    turns = np.mod(
        np.arange(SUB)[None, :] * (2 * np.arange(facets)[:, None] + 1), 2 * facets
    )
    angle = turns * (np.pi / facets)
    return np.cos(angle).astype(np.float32), np.sin(angle).astype(np.float32)


def offset_tables(offsets_ref, position, width):
    subgrids = offsets_ref.shape[1]
    image_width = width * subgrids
    down = lax.broadcasted_iota(jnp.int32, (subgrids, subgrids), 0)
    across = lax.broadcasted_iota(jnp.int32, (subgrids, subgrids), 1)
    column = jnp.sum(jnp.where(down == across, offsets_ref[...], 0), axis=1, keepdims=True)
    lane = lax.broadcasted_iota(jnp.int32, (subgrids, LANES), 1)

    def parts(product, modulus):
        whole = jnp.floor(product.astype(jnp.float32) * (1.0 / modulus)).astype(jnp.int32)
        angle = (product - whole * modulus).astype(jnp.float32) * (two_pi / modulus)
        return jnp.cos(angle), jnp.sin(angle)

    facet_turns = jnp.bitwise_and(column * position, subgrids - 1)
    return {
        "start": parts(column * (position * (width // LANES) + lane), image_width // LANES),
        "cell": parts(column * lane, image_width),
        "tile": parts(column * lane, image_width // LANES),
        "inner": parts(column * (2 * lane + 1), 2 * image_width),
        "middle": parts(
            column * (width - 1) + 2 * width * facet_turns + 0 * lane, 2 * image_width
        ),
    }


def encode_kernel(
    slab_hbm, window_hbm, offsets_ref, coarse_hbm, fine_hbm, turn_hbm, flip_hbm, out_ref, tables_ref,
    slab_ref, window_ref, coarse_ref, fine_ref, turn_ref, flip_ref,
    phase_ref, side_ref, turn_table_ref, wave_ref, total_ref, sems,
):
    columns = slab_ref.shape[0] // 2
    width = slab_ref.shape[1]
    half = width // 2
    subgrids = offsets_ref.shape[1]
    rows = CONTRIB // FINE
    pairs = (
        (slab_hbm, slab_ref), (window_hbm, window_ref), (coarse_hbm, coarse_ref),
        (fine_hbm, fine_ref), (turn_hbm, turn_ref), (flip_hbm, flip_ref),
    )
    copies = [pltpu.make_async_copy(a, b, sems.at[n]) for n, (a, b) in enumerate(pairs)]
    for copy in copies:
        copy.start()
    turns = offset_tables(offsets_ref, lax.axis_index("facet"), width)
    for n in range(2):
        tables_ref[n] = turns["start"][n]
        tables_ref[2 + n] = turns["cell"][n]
    high, low, centre = turns["tile"], turns["inner"], turns["middle"]
    for tile in range(half // LANES):
        c, s = high[0][:, tile : tile + 1], high[1][:, tile : tile + 1]
        span = slice(tile * LANES, (tile + 1) * LANES)
        phase_ref[0, :, span] = c * low[0] - s * low[1]
        phase_ref[1, :, span] = s * low[0] + c * low[1]
    for copy in copies:
        copy.wait()

    def windowed(span):
        product = slab_ref[:, span].astype(jnp.float32) * window_ref[:, span]
        return product.astype(jnp.bfloat16)

    def stage_columns(tile, fine):
        span = slice(tile * STEP, (tile + 1) * STEP)
        slot = tile % 2
        if fine == 0:
            side_ref[0] = windowed(
                slice(half + tile * STEP, half + (tile + 1) * STEP)
            ).astype(jnp.float32)
            side_ref[1] = lax.dot_general(
                windowed(slice(half - (tile + 1) * STEP, half - tile * STEP)), flip_ref[...], NN,
                preferred_element_type=jnp.float32,
            )
        sides = []
        for n in range(2):
            re, im = side_ref[n, :columns], side_ref[n, columns:]
            if fine > 0:
                row = (2 * fine + n) * 2
                c, s = fine_ref[row : row + 1, span], fine_ref[row + 1 : row + 2, span]
                re, im = re * c + im * s, im * c - re * s
            sides.append((re, im))
        (re_p, im_p), (re_m, im_m) = sides
        upper = slice(2 * columns * fine, 2 * columns * fine + columns)
        lower = slice(2 * columns * fine + columns, 2 * columns * (fine + 1))
        wave_ref[slot, upper, :STEP] = (re_p + re_m).astype(jnp.bfloat16)
        wave_ref[slot, lower, :STEP] = (im_p + im_m).astype(jnp.bfloat16)
        wave_ref[slot, upper, STEP:] = (im_p - im_m).astype(jnp.bfloat16)
        wave_ref[slot, lower, STEP:] = (re_m - re_p).astype(jnp.bfloat16)

    def stage_rows(tile, s):
        span = slice(tile * STEP, (tile + 1) * STEP)
        where = slice(s * rows, (s + 1) * rows)
        cj, sj = coarse_ref[0, :, span], coarse_ref[1, :, span]
        co, so = phase_ref[0, s : s + 1, span], phase_ref[1, s : s + 1, span]
        turn_table_ref[tile % 2, where, :STEP] = (co * cj - so * sj).astype(jnp.bfloat16)
        turn_table_ref[tile % 2, where, STEP:] = (so * cj + co * sj).astype(jnp.bfloat16)

    cm, sm = turn_ref[0], turn_ref[1]
    scale = width ** (-0.5)
    sign = jnp.where(
        lax.broadcasted_iota(jnp.int32, (1, 2 * columns), 1) < columns, scale, -scale
    )

    def finish(s):
        co, so = centre[0][s : s + 1], centre[1][s : s + 1]
        c = (co * cm + so * sm) * scale
        d = (so * cm - co * sm) * sign
        blocks = []
        for fine in range(FINE):
            block = total_ref[s * rows : (s + 1) * rows, fine * LANES : (fine + 1) * LANES]
            blocks.append(block * c + pltpu.roll(block, columns, 1) * d)
        out_ref[s] = jnp.concatenate(blocks, 0).T.astype(jnp.bfloat16)

    steps = half // STEP
    each = subgrids // BLOCKS
    for fine in range(FINE):
        stage_columns(0, fine)
    for s in range(subgrids):
        stage_rows(0, s)
    for tile in range(steps):
        for block in range(BLOCKS):
            where = slice(block * each * rows, (block + 1) * each * rows)
            part = lax.dot_general(
                turn_table_ref[tile % 2, where], wave_ref[tile % 2], NT,
                preferred_element_type=jnp.float32,
            )
            if tile == 0:
                total_ref[where] = part
            else:
                total_ref[where] += part
            if tile + 1 < steps:
                for fine in range(block * FINE // BLOCKS, (block + 1) * FINE // BLOCKS):
                    stage_columns(tile + 1, fine)
                for s in range(block * each, (block + 1) * each):
                    stage_rows(tile + 1, s)
            else:
                for s in range(block * each, (block + 1) * each):
                    finish(s)


def grid_kernel(
    recv_ref, kernel_ref, cos_ref, sin_ref, counts_ref, part_ref, out_ref, re_ref, im_ref
):
    facets = recv_ref.shape[0]
    columns = recv_ref.shape[1] // 2
    cells = re_ref.shape[1]
    half = facets // 2
    re_ref[...] = jnp.zeros_like(re_ref)
    im_ref[...] = jnp.zeros_like(im_ref)

    for f in range(facets // 4):
        first, second, third, fourth = (
            recv_ref[n].astype(jnp.float32) for n in (f, f + half, facets - 1 - f, half - 1 - f)
        )
        for parity in range(2):
            span = slice(parity * cells // 2, (parity + 1) * cells // 2)
            near = first + second if parity == 0 else first - second
            far = third + fourth if parity == 0 else third - fourth
            both = jnp.concatenate([near + far, near - far], 0).astype(jnp.bfloat16)
            wide = lax.dot_general(
                both, kernel_ref[:, span], NN, preferred_element_type=jnp.float32
            )
            even_re, even_im = wide[:columns], wide[columns : 2 * columns]
            odd_re, odd_im = wide[2 * columns : 3 * columns], wide[3 * columns :]
            c, s = cos_ref[f : f + 1, span], sin_ref[f : f + 1, span]
            re_ref[:, span] += even_re * c + odd_im * s
            im_ref[:, span] += even_im * c - odd_re * s

    counts = lax.dot_general(
        counts_ref[...].astype(jnp.float32).astype(jnp.bfloat16), part_ref[...], NN,
        preferred_element_type=jnp.float32,
    )
    weights = jnp.where(counts > 0, 1.0 / jnp.maximum(counts, 1.0), 0.0) * (
        (2 * facets) ** (-0.5)
    )
    re = re_ref[...] * weights
    im = im_ref[...] * weights
    per = out_ref.shape[1] // 2
    for layer in range(out_ref.shape[0]):
        span = slice(layer * per, (layer + 1) * per)
        out_ref[layer] = jnp.concatenate([re[span], im[span]], 0).astype(jnp.bfloat16)


def back_kernel(recv_ref, kernel_ref, cos_ref, sin_ref, out_ref, rows_ref):
    layers = recv_ref.shape[0]
    facets = out_ref.shape[0]
    total = recv_ref[0].astype(jnp.float32)
    for layer in range(1, layers):
        total = total + recv_ref[layer].astype(jnp.float32)
    per = total.shape[0] // 2
    re, im = total[:per], total[per:]
    for f in range(facets):
        c = cos_ref[f : f + 1, :]
        s = sin_ref[f : f + 1, :]
        turned = jnp.concatenate([re * c - im * s, im * c + re * s], 0)
        rows_ref[f * 2 * per : (f + 1) * 2 * per, :] = turned.astype(jnp.bfloat16)
    back = lax.dot_general(
        rows_ref[...], kernel_ref[...], NT, preferred_element_type=jnp.float32
    )
    out_ref[...] = (back * 0.5).astype(jnp.bfloat16).reshape(out_ref.shape)


def decode_kernel(
    recv_ref, window_ref, tables_ref, table_ref, out_ref, pr_ref, pi_ref
):
    subgrids = recv_ref.shape[0]
    per = recv_ref.shape[1] // 2
    width = out_ref.shape[2]
    for tile in range(width // LANES):
        c, s = tables_ref[0, :, tile : tile + 1], tables_ref[1, :, tile : tile + 1]
        span = slice(tile * LANES, (tile + 1) * LANES)
        pr_ref[:, span] = c * tables_ref[2] - s * tables_ref[3]
        pi_ref[:, span] = s * tables_ref[2] + c * tables_ref[3]
    rows = recv_ref[...].astype(jnp.float32)
    re, im = rows[:, :per], rows[:, per:]
    left_re = jnp.concatenate([re, im], 2).reshape(subgrids * per, 2 * CONTRIB).astype(jnp.bfloat16)
    left_im = jnp.concatenate([im, -re], 2).reshape(subgrids * per, 2 * CONTRIB).astype(jnp.bfloat16)
    scale = (subgrids * CONTRIB) ** (-0.5)
    for tile in range(width // 256):
        span = slice(tile * 256, (tile + 1) * 256)
        table = table_ref[:, span]
        zr = lax.dot_general(left_re, table, NN, preferred_element_type=jnp.float32)
        zi = lax.dot_general(left_im, table, NN, preferred_element_type=jnp.float32)
        out_re, out_im = None, None
        for s in range(subgrids):
            a = zr[s * per : (s + 1) * per]
            b = zi[s * per : (s + 1) * per]
            pr = pr_ref[s : s + 1, span]
            pi = pi_ref[s : s + 1, span]
            re_term = pr * a - pi * b
            im_term = pr * b + pi * a
            out_re = re_term if out_re is None else out_re + re_term
            out_im = im_term if out_im is None else out_im + im_term
        taper = window_ref[:, span] * scale
        out_ref[0, :, span] = out_re * taper
        out_ref[1, :, span] = out_im * taper


def params(mebibytes):
    return pltpu.CompilerParams(vmem_limit_bytes=mebibytes * 2**20)


def shards(slabs, window, density, offsets):
    layers = lax.axis_size("layer")
    facets = lax.axis_size("facet")
    columns, width = slabs.shape[2], slabs.shape[3]
    per = columns // layers
    sample_step = SUB // CONTRIB
    image_width = width * facets
    table = jnp.asarray(step_table(width, image_width, sample_step))
    folds = [jnp.asarray(part) for part in fold_tables(width, image_width, sample_step)]
    cells = np.concatenate([np.arange(0, SUB, 2), np.arange(1, SUB, 2)])
    spreading = np.ascontiguousarray(kernel_table(sample_step)[:, cells])
    parting = np.eye(SUB)[:, cells].astype(ml_dtypes.bfloat16)
    spread = jnp.asarray(spreading)
    order = np.arange(CONTRIB).reshape(CONTRIB // FINE, FINE).T.reshape(-1)
    spread_in = jnp.asarray(np.ascontiguousarray(spreading[order]))
    cos_u, sin_u = (
        jnp.asarray(np.ascontiguousarray(part[:, cells])) for part in centre_phases(facets)
    )

    window_row = window.reshape(1, width)

    whole = pl.BlockSpec(memory_space=pltpu.VMEM)
    anywhere = pl.BlockSpec(memory_space=pl.ANY)
    rows = facets * CONTRIB // FINE
    wide = 2 * columns * FINE
    half = width // 2
    outgoing, tables = pl.pallas_call(
        encode_kernel,
        out_shape=(
            jax.ShapeDtypeStruct((facets, 2 * columns, CONTRIB), jnp.bfloat16),
            jax.ShapeDtypeStruct((4, facets, LANES), jnp.float32),
        ),
        in_specs=[anywhere, anywhere, whole] + [anywhere] * 4,
        out_specs=(whole, whole),
        scratch_shapes=[
            pltpu.VMEM((2 * columns, width), jnp.bfloat16),
            pltpu.VMEM((1, width), jnp.float32),
            pltpu.VMEM((2, CONTRIB // FINE, half), jnp.float32),
            pltpu.VMEM((4 * FINE, half), jnp.float32),
            pltpu.VMEM((2, CONTRIB // FINE, LANES), jnp.float32),
            pltpu.VMEM((STEP, STEP), jnp.bfloat16),
            pltpu.VMEM((2, facets, half), jnp.float32),
            pltpu.VMEM((2, 2 * columns, STEP), jnp.float32),
            pltpu.VMEM((2, rows, 2 * STEP), jnp.bfloat16),
            pltpu.VMEM((2, wide, 2 * STEP), jnp.bfloat16),
            pltpu.VMEM((rows, wide), jnp.float32),
            pltpu.SemaphoreType.DMA((6,)),
        ],
        compiler_params=params(60),
        name="encode",
    )(slabs.reshape(2 * columns, width), window_row, offsets.reshape(1, facets), *folds)

    received = lax.all_to_all(outgoing, "facet", split_axis=0, concat_axis=0, tiled=True)

    gridded = pl.pallas_call(
        grid_kernel,
        out_shape=jax.ShapeDtypeStruct((layers, 2 * per, SUB), jnp.bfloat16),
        in_specs=[whole] * 6,
        out_specs=whole,
        scratch_shapes=[pltpu.VMEM((columns, SUB), jnp.float32)] * 2,
        compiler_params=params(48),
        name="subgrid",
    )(received, spread_in, cos_u, sin_u, density[0], jnp.asarray(parting))

    by_layer = lax.all_to_all(gridded, "layer", split_axis=0, concat_axis=0, tiled=True)

    back_out = pl.pallas_call(
        back_kernel,
        out_shape=jax.ShapeDtypeStruct((facets, 2 * per, CONTRIB), jnp.bfloat16),
        in_specs=[whole] * 4,
        out_specs=whole,
        scratch_shapes=[pltpu.VMEM((facets * 2 * per, SUB), jnp.bfloat16)],
        compiler_params=params(48),
        name="back",
    )(by_layer, spread, cos_u, sin_u)

    returned = lax.all_to_all(back_out, "facet", split_axis=0, concat_axis=0, tiled=True)

    return pl.pallas_call(
        decode_kernel,
        out_shape=jax.ShapeDtypeStruct((2, per, width), jnp.float32),
        in_specs=[whole] * 4,
        out_specs=whole,
        scratch_shapes=[pltpu.VMEM((facets, width), jnp.float32)] * 2,
        compiler_params=params(48),
        name="decode",
    )(returned, window_row, tables, table)


def solution(mesh):
    placed = (P("layer", None, None, "facet"), P("facet"), P("layer", None, "facet"), P())
    return jax.shard_map(
        shards, mesh=mesh, in_specs=placed, out_specs=P(None, "layer", "facet"), check_vma=False
    )
```

```python
import math

import jax
import jax.numpy as jnp
import ml_dtypes
import numpy as np
from jax import lax
from jax.experimental import pallas as pl
from jax.experimental.pallas import tpu as pltpu
from jax.sharding import PartitionSpec as P

CONTRIB = 128
SUB = 512
LANES = 128
FINE = 4
STEP = 256
BLOCKS = 2

two_pi = 2.0 * math.pi
NT = (((1,), (1,)), ((), ()))
NN = (((1,), (0,)), ((), ()))


def step_table(facet_width, image_width, sample_step):
    j = np.arange(CONTRIB, dtype=np.int64)[:, None]
    cell = np.arange(facet_width, dtype=np.int64)[None, :] - facet_width // 2
    angle = np.mod(sample_step * j * cell, image_width) * (-2.0 * np.pi / image_width)
    return np.concatenate([np.cos(angle), np.sin(angle)], 0).astype(ml_dtypes.bfloat16)


def fold_tables(facet_width, image_width, sample_step):
    k = np.arange(facet_width // 2, dtype=np.int64)[None, :]
    j1 = np.arange(CONTRIB // FINE, dtype=np.int64)[:, None]
    j2 = np.arange(FINE, dtype=np.int64)[:, None]

    def parts(turns):
        angle = np.mod(turns, image_width) * (2.0 * np.pi / image_width)
        return np.stack([np.cos(angle), np.sin(angle)]).astype(np.float32)

    half_step = sample_step * FINE // 2
    coarse = parts(half_step * j1 * (2 * k + 1))
    fine = np.stack([parts(sample_step * j2 * k), parts(-sample_step * j2 * (k + 1))])
    fine = fine.transpose(2, 0, 1, 3).reshape(4 * FINE, facet_width // 2)
    turn = np.broadcast_to(parts(half_step * j1), (2, CONTRIB // FINE, LANES))
    flip = np.eye(STEP)[::-1].astype(ml_dtypes.bfloat16)
    return coarse, np.ascontiguousarray(fine), np.ascontiguousarray(turn), np.ascontiguousarray(flip)


def kernel_table(sample_step):
    spacing = np.arange(SUB)[None, :] - sample_step * np.arange(CONTRIB)[:, None]
    scaled = spacing / sample_step
    return (1.0 / (1.0 + scaled * scaled)).astype(ml_dtypes.bfloat16)


def centre_phases(facets):
    turns = np.mod(
        np.arange(SUB)[None, :] * (2 * np.arange(facets)[:, None] + 1), 2 * facets
    )
    angle = turns * (np.pi / facets)
    return np.cos(angle).astype(np.float32), np.sin(angle).astype(np.float32)


def offset_tables(offsets_ref, position, width):
    subgrids = offsets_ref.shape[1]
    image_width = width * subgrids
    down = lax.broadcasted_iota(jnp.int32, (subgrids, subgrids), 0)
    across = lax.broadcasted_iota(jnp.int32, (subgrids, subgrids), 1)
    column = jnp.sum(jnp.where(down == across, offsets_ref[...], 0), axis=1, keepdims=True)
    lane = lax.broadcasted_iota(jnp.int32, (subgrids, LANES), 1)

    def parts(product, modulus):
        whole = jnp.floor(product.astype(jnp.float32) * (1.0 / modulus)).astype(jnp.int32)
        angle = (product - whole * modulus).astype(jnp.float32) * (two_pi / modulus)
        return jnp.cos(angle), jnp.sin(angle)

    facet_turns = jnp.bitwise_and(column * position, subgrids - 1)
    return {
        "start": parts(column * (position * (width // LANES) + lane), image_width // LANES),
        "cell": parts(column * lane, image_width),
        "tile": parts(column * lane, image_width // LANES),
        "inner": parts(column * (2 * lane + 1), 2 * image_width),
        "middle": parts(
            column * (width - 1) + 2 * width * facet_turns + 0 * lane, 2 * image_width
        ),
    }


def encode_kernel(
    slab_hbm, window_hbm, offsets_ref, coarse_hbm, fine_hbm, turn_hbm, flip_hbm, out_ref, tables_ref,
    slab_ref, window_ref, coarse_ref, fine_ref, turn_ref, flip_ref,
    phase_ref, side_ref, turn_table_ref, wave_ref, total_ref, sems,
):
    columns = slab_ref.shape[0] // 2
    width = slab_ref.shape[1]
    half = width // 2
    subgrids = offsets_ref.shape[1]
    rows = CONTRIB // FINE
    pairs = (
        (slab_hbm, slab_ref), (window_hbm, window_ref), (coarse_hbm, coarse_ref),
        (fine_hbm, fine_ref), (turn_hbm, turn_ref), (flip_hbm, flip_ref),
    )
    copies = [pltpu.make_async_copy(a, b, sems.at[n]) for n, (a, b) in enumerate(pairs)]
    for copy in copies:
        copy.start()
    turns = offset_tables(offsets_ref, lax.axis_index("facet"), width)
    for n in range(2):
        tables_ref[n] = turns["start"][n]
        tables_ref[2 + n] = turns["cell"][n]
    high, low, centre = turns["tile"], turns["inner"], turns["middle"]
    for tile in range(half // LANES):
        c, s = high[0][:, tile : tile + 1], high[1][:, tile : tile + 1]
        span = slice(tile * LANES, (tile + 1) * LANES)
        phase_ref[0, :, span] = c * low[0] - s * low[1]
        phase_ref[1, :, span] = s * low[0] + c * low[1]
    for copy in copies:
        copy.wait()

    def windowed(span):
        product = slab_ref[:, span].astype(jnp.float32) * window_ref[:, span]
        return product.astype(jnp.bfloat16)

    def stage_columns(tile, fine):
        span = slice(tile * STEP, (tile + 1) * STEP)
        slot = tile % 2
        if fine == 0:
            side_ref[0] = windowed(
                slice(half + tile * STEP, half + (tile + 1) * STEP)
            ).astype(jnp.float32)
            side_ref[1] = lax.dot_general(
                windowed(slice(half - (tile + 1) * STEP, half - tile * STEP)), flip_ref[...], NN,
                preferred_element_type=jnp.float32,
            )
        sides = []
        for n in range(2):
            re, im = side_ref[n, :columns], side_ref[n, columns:]
            if fine > 0:
                row = (2 * fine + n) * 2
                c, s = fine_ref[row : row + 1, span], fine_ref[row + 1 : row + 2, span]
                re, im = re * c + im * s, im * c - re * s
            sides.append((re, im))
        (re_p, im_p), (re_m, im_m) = sides
        upper = slice(2 * columns * fine, 2 * columns * fine + columns)
        lower = slice(2 * columns * fine + columns, 2 * columns * (fine + 1))
        wave_ref[slot, upper, :STEP] = (re_p + re_m).astype(jnp.bfloat16)
        wave_ref[slot, lower, :STEP] = (im_p + im_m).astype(jnp.bfloat16)
        wave_ref[slot, upper, STEP:] = (im_p - im_m).astype(jnp.bfloat16)
        wave_ref[slot, lower, STEP:] = (re_m - re_p).astype(jnp.bfloat16)

    def stage_rows(tile, s):
        span = slice(tile * STEP, (tile + 1) * STEP)
        where = slice(s * rows, (s + 1) * rows)
        cj, sj = coarse_ref[0, :, span], coarse_ref[1, :, span]
        co, so = phase_ref[0, s : s + 1, span], phase_ref[1, s : s + 1, span]
        turn_table_ref[tile % 2, where, :STEP] = (co * cj - so * sj).astype(jnp.bfloat16)
        turn_table_ref[tile % 2, where, STEP:] = (so * cj + co * sj).astype(jnp.bfloat16)

    cm, sm = turn_ref[0], turn_ref[1]
    scale = width ** (-0.5)
    sign = jnp.where(
        lax.broadcasted_iota(jnp.int32, (1, 2 * columns), 1) < columns, scale, -scale
    )

    def finish(s):
        co, so = centre[0][s : s + 1], centre[1][s : s + 1]
        c = (co * cm + so * sm) * scale
        d = (so * cm - co * sm) * sign
        blocks = []
        for fine in range(FINE):
            block = total_ref[s * rows : (s + 1) * rows, fine * LANES : (fine + 1) * LANES]
            blocks.append(block * c + pltpu.roll(block, columns, 1) * d)
        down = jnp.concatenate(blocks, 0).T
        per = out_ref.shape[2] // 2
        for layer in range(out_ref.shape[0]):
            first = layer * per
            out_ref[layer, s] = jnp.concatenate(
                [down[first : first + per], down[columns + first : columns + first + per]], 0
            ).astype(jnp.bfloat16)

    steps = half // STEP
    each = subgrids // BLOCKS
    for fine in range(FINE):
        stage_columns(0, fine)
    for s in range(subgrids):
        stage_rows(0, s)
    for tile in range(steps):
        for block in range(BLOCKS):
            where = slice(block * each * rows, (block + 1) * each * rows)
            part = lax.dot_general(
                turn_table_ref[tile % 2, where], wave_ref[tile % 2], NT,
                preferred_element_type=jnp.float32,
            )
            if tile == 0:
                total_ref[where] = part
            else:
                total_ref[where] += part
            if tile + 1 < steps:
                for fine in range(block * FINE // BLOCKS, (block + 1) * FINE // BLOCKS):
                    stage_columns(tile + 1, fine)
                for s in range(block * each, (block + 1) * each):
                    stage_rows(tile + 1, s)
            else:
                for s in range(block * each, (block + 1) * each):
                    finish(s)


def subgrid_kernel(
    recv_ref, kernel_ref, cos_ref, sin_ref, counts_ref, part_ref, back_ref, out_ref,
    re_ref, im_ref, rows_ref,
):
    layers, facets, tall, contrib = recv_ref.shape
    per = tall // 2
    cells = re_ref.shape[1]
    half = facets // 2
    for f in range(facets // 4):
        first, second, third, fourth = (
            recv_ref[:, n].astype(jnp.float32)
            for n in (f, f + half, facets - 1 - f, half - 1 - f)
        )
        for parity in range(2):
            span = slice(parity * cells // 2, (parity + 1) * cells // 2)
            near = first + second if parity == 0 else first - second
            far = third + fourth if parity == 0 else third - fourth
            both = jnp.concatenate([near + far, near - far], 0)
            wide = lax.dot_general(
                both.reshape(2 * layers * tall, contrib).astype(jnp.bfloat16),
                kernel_ref[:, span], NN, preferred_element_type=jnp.float32,
            ).reshape(2, layers, 2, per, cells // 2)
            even_re, even_im, odd_re, odd_im = (
                wide[a, :, b].reshape(layers * per, cells // 2) for a in range(2) for b in range(2)
            )
            c, s = cos_ref[f : f + 1, span], sin_ref[f : f + 1, span]
            re = even_re * c + odd_im * s
            im = even_im * c - odd_re * s
            if f == 0:
                re_ref[:, span] = re
                im_ref[:, span] = im
            else:
                re_ref[:, span] += re
                im_ref[:, span] += im
    counts = lax.dot_general(
        counts_ref[...].reshape(layers * per, cells).astype(jnp.float32).astype(jnp.bfloat16),
        part_ref[...], NN, preferred_element_type=jnp.float32,
    )
    weights = jnp.where(counts > 0, 1.0 / jnp.maximum(counts, 1.0), 0.0) * (
        (2 * facets) ** (-0.5)
    )
    re = jnp.sum((re_ref[...] * weights).reshape(layers, per, cells), axis=0)
    im = jnp.sum((im_ref[...] * weights).reshape(layers, per, cells), axis=0)
    for f in range(facets):
        c, s = cos_ref[f : f + 1, :], sin_ref[f : f + 1, :]
        turned = jnp.concatenate([re * c - im * s, im * c + re * s], 0)
        rows_ref[f * tall : (f + 1) * tall, :] = turned.astype(jnp.bfloat16)
    back = lax.dot_general(
        rows_ref[...], back_ref[...], NT, preferred_element_type=jnp.float32
    )
    out_ref[...] = (back * 0.5).astype(jnp.bfloat16).reshape(out_ref.shape)


def decode_kernel(
    recv_ref, window_ref, tables_ref, table_ref, out_ref, pr_ref, pi_ref
):
    subgrids = recv_ref.shape[0]
    per = recv_ref.shape[1] // 2
    width = out_ref.shape[2]
    for tile in range(width // LANES):
        c, s = tables_ref[0, :, tile : tile + 1], tables_ref[1, :, tile : tile + 1]
        span = slice(tile * LANES, (tile + 1) * LANES)
        pr_ref[:, span] = c * tables_ref[2] - s * tables_ref[3]
        pi_ref[:, span] = s * tables_ref[2] + c * tables_ref[3]
    rows = recv_ref[...].astype(jnp.float32)
    re, im = rows[:, :per], rows[:, per:]
    left_re = jnp.concatenate([re, im], 2).reshape(subgrids * per, 2 * CONTRIB).astype(jnp.bfloat16)
    left_im = jnp.concatenate([im, -re], 2).reshape(subgrids * per, 2 * CONTRIB).astype(jnp.bfloat16)
    scale = (subgrids * CONTRIB) ** (-0.5)
    for tile in range(width // 256):
        span = slice(tile * 256, (tile + 1) * 256)
        table = table_ref[:, span]
        zr = lax.dot_general(left_re, table, NN, preferred_element_type=jnp.float32)
        zi = lax.dot_general(left_im, table, NN, preferred_element_type=jnp.float32)
        out_re, out_im = None, None
        for s in range(subgrids):
            a = zr[s * per : (s + 1) * per]
            b = zi[s * per : (s + 1) * per]
            pr = pr_ref[s : s + 1, span]
            pi = pi_ref[s : s + 1, span]
            re_term = pr * a - pi * b
            im_term = pr * b + pi * a
            out_re = re_term if out_re is None else out_re + re_term
            out_im = im_term if out_im is None else out_im + im_term
        taper = window_ref[:, span] * scale
        out_ref[0, :, span] = out_re * taper
        out_ref[1, :, span] = out_im * taper


def params(mebibytes):
    return pltpu.CompilerParams(vmem_limit_bytes=mebibytes * 2**20)


def shards(slabs, window, density, offsets):
    layers = lax.axis_size("layer")
    facets = lax.axis_size("facet")
    columns, width = slabs.shape[2], slabs.shape[3]
    per = columns // layers
    sample_step = SUB // CONTRIB
    image_width = width * facets
    table = jnp.asarray(step_table(width, image_width, sample_step))
    folds = [jnp.asarray(part) for part in fold_tables(width, image_width, sample_step)]
    cells = np.concatenate([np.arange(0, SUB, 2), np.arange(1, SUB, 2)])
    spreading = np.ascontiguousarray(kernel_table(sample_step)[:, cells])
    parting = np.eye(SUB)[:, cells].astype(ml_dtypes.bfloat16)
    spread = jnp.asarray(spreading)
    order = np.arange(CONTRIB).reshape(CONTRIB // FINE, FINE).T.reshape(-1)
    spread_in = jnp.asarray(np.ascontiguousarray(spreading[order]))
    cos_u, sin_u = (
        jnp.asarray(np.ascontiguousarray(part[:, cells])) for part in centre_phases(facets)
    )

    window_row = window.reshape(1, width)

    whole = pl.BlockSpec(memory_space=pltpu.VMEM)
    counts = lax.all_to_all(
        density.reshape(layers, per, SUB), "layer", split_axis=0, concat_axis=0, tiled=True
    )
    anywhere = pl.BlockSpec(memory_space=pl.ANY)
    rows = facets * CONTRIB // FINE
    wide = 2 * columns * FINE
    half = width // 2
    outgoing, tables = pl.pallas_call(
        encode_kernel,
        out_shape=(
            jax.ShapeDtypeStruct((layers, facets, 2 * per, CONTRIB), jnp.bfloat16),
            jax.ShapeDtypeStruct((4, facets, LANES), jnp.float32),
        ),
        in_specs=[anywhere, anywhere, whole] + [anywhere] * 4,
        out_specs=(whole, whole),
        scratch_shapes=[
            pltpu.VMEM((2 * columns, width), jnp.bfloat16),
            pltpu.VMEM((1, width), jnp.float32),
            pltpu.VMEM((2, CONTRIB // FINE, half), jnp.float32),
            pltpu.VMEM((4 * FINE, half), jnp.float32),
            pltpu.VMEM((2, CONTRIB // FINE, LANES), jnp.float32),
            pltpu.VMEM((STEP, STEP), jnp.bfloat16),
            pltpu.VMEM((2, facets, half), jnp.float32),
            pltpu.VMEM((2, 2 * columns, STEP), jnp.float32),
            pltpu.VMEM((2, rows, 2 * STEP), jnp.bfloat16),
            pltpu.VMEM((2, wide, 2 * STEP), jnp.bfloat16),
            pltpu.VMEM((rows, wide), jnp.float32),
            pltpu.SemaphoreType.DMA((6,)),
        ],
        compiler_params=params(60),
        cost_estimate=pl.CostEstimate(
            flops=4 * rows * half * wide, bytes_accessed=4 * width * rows, transcendentals=0
        ),
        name="encode",
    )(slabs.reshape(2 * columns, width), window_row, offsets.reshape(1, facets), *folds)

    outgoing, counts = lax.optimization_barrier((outgoing, counts))
    received = lax.all_to_all(
        outgoing.reshape(layers * facets, 2 * per, CONTRIB), ("layer", "facet"),
        split_axis=0, concat_axis=0, tiled=True,
    ).reshape(layers, facets, 2 * per, CONTRIB)

    back_out = pl.pallas_call(
        subgrid_kernel,
        out_shape=jax.ShapeDtypeStruct((facets, 2 * per, CONTRIB), jnp.bfloat16),
        in_specs=[whole] * 7,
        out_specs=whole,
        scratch_shapes=[
            pltpu.VMEM((columns, SUB), jnp.float32),
            pltpu.VMEM((columns, SUB), jnp.float32),
            pltpu.VMEM((facets * 2 * per, SUB), jnp.bfloat16),
        ],
        compiler_params=params(48),
        name="subgrid",
    )(received, spread_in, cos_u, sin_u, counts, jnp.asarray(parting), spread)

    returned = lax.all_to_all(back_out, "facet", split_axis=0, concat_axis=0, tiled=True)

    return pl.pallas_call(
        decode_kernel,
        out_shape=jax.ShapeDtypeStruct((2, per, width), jnp.float32),
        in_specs=[whole] * 4,
        out_specs=whole,
        scratch_shapes=[pltpu.VMEM((facets, width), jnp.float32)] * 2,
        compiler_params=params(48),
        name="decode",
    )(returned, window_row, tables, table)


def solution(mesh):
    placed = (P("layer", None, None, "facet"), P("facet"), P("layer", None, "facet"), P())
    return jax.shard_map(
        shards, mesh=mesh, in_specs=placed, out_specs=P(None, "layer", "facet"), check_vma=False
    )
```

```python
import math

import jax
import jax.numpy as jnp
import ml_dtypes
import numpy as np
from jax import lax
from jax.experimental import pallas as pl
from jax.experimental.pallas import tpu as pltpu
from jax.sharding import PartitionSpec as P

CONTRIB = 128
SUB = 512
LANES = 128
FINE = 4
STEP = 256
BLOCKS = 2

two_pi = 2.0 * math.pi
NT = (((1,), (1,)), ((), ()))
NN = (((1,), (0,)), ((), ()))


def step_table(facet_width, image_width, sample_step):
    j = np.arange(CONTRIB, dtype=np.int64)[:, None]
    cell = np.arange(facet_width, dtype=np.int64)[None, :] - facet_width // 2
    angle = np.mod(sample_step * j * cell, image_width) * (-2.0 * np.pi / image_width)
    return np.concatenate([np.cos(angle), np.sin(angle)], 0).astype(ml_dtypes.bfloat16)


def fold_tables(facet_width, image_width, sample_step):
    k = np.arange(facet_width // 2, dtype=np.int64)[None, :]
    j1 = np.arange(CONTRIB // FINE, dtype=np.int64)[:, None]
    j2 = np.arange(FINE, dtype=np.int64)[:, None]

    def parts(turns):
        angle = np.mod(turns, image_width) * (2.0 * np.pi / image_width)
        return np.stack([np.cos(angle), np.sin(angle)]).astype(np.float32)

    half_step = sample_step * FINE // 2
    coarse = parts(half_step * j1 * (2 * k + 1))
    fine = np.stack([parts(sample_step * j2 * k), parts(-sample_step * j2 * (k + 1))])
    fine = fine.transpose(2, 0, 1, 3).reshape(4 * FINE, facet_width // 2)
    turn = np.broadcast_to(parts(half_step * j1), (2, CONTRIB // FINE, LANES))
    flip = np.eye(STEP)[::-1].astype(ml_dtypes.bfloat16)
    return coarse, np.ascontiguousarray(fine), np.ascontiguousarray(turn), np.ascontiguousarray(flip)


def kernel_table(sample_step):
    spacing = np.arange(SUB)[None, :] - sample_step * np.arange(CONTRIB)[:, None]
    scaled = spacing / sample_step
    return (1.0 / (1.0 + scaled * scaled)).astype(ml_dtypes.bfloat16)


def centre_phases(facets):
    turns = np.mod(
        np.arange(SUB)[None, :] * (2 * np.arange(facets)[:, None] + 1), 2 * facets
    )
    angle = turns * (np.pi / facets)
    return np.cos(angle).astype(np.float32), np.sin(angle).astype(np.float32)


def offset_tables(offsets_ref, position, width):
    subgrids = offsets_ref.shape[1]
    image_width = width * subgrids
    down = lax.broadcasted_iota(jnp.int32, (subgrids, subgrids), 0)
    across = lax.broadcasted_iota(jnp.int32, (subgrids, subgrids), 1)
    column = jnp.sum(jnp.where(down == across, offsets_ref[...], 0), axis=1, keepdims=True)
    lane = lax.broadcasted_iota(jnp.int32, (subgrids, LANES), 1)

    def parts(product, modulus):
        whole = jnp.floor(product.astype(jnp.float32) * (1.0 / modulus)).astype(jnp.int32)
        angle = (product - whole * modulus).astype(jnp.float32) * (two_pi / modulus)
        return jnp.cos(angle), jnp.sin(angle)

    facet_turns = jnp.bitwise_and(column * position, subgrids - 1)
    return {
        "start": parts(column * (position * (width // LANES) + lane), image_width // LANES),
        "cell": parts(column * lane, image_width),
        "tile": parts(column * lane, image_width // LANES),
        "inner": parts(column * (2 * lane + 1), 2 * image_width),
        "middle": parts(
            column * (width - 1) + 2 * width * facet_turns + 0 * lane, 2 * image_width
        ),
    }


def encode_kernel(
    slab_hbm, window_hbm, offsets_ref, coarse_hbm, fine_hbm, turn_hbm, flip_hbm, out_ref, tables_ref,
    slab_ref, window_ref, coarse_ref, fine_ref, turn_ref, flip_ref,
    phase_ref, side_ref, turn_table_ref, wave_ref, total_ref, sems,
):
    columns = slab_ref.shape[0] // 2
    width = slab_ref.shape[1]
    half = width // 2
    subgrids = offsets_ref.shape[1]
    rows = CONTRIB // FINE
    pairs = (
        (slab_hbm, slab_ref), (window_hbm, window_ref), (coarse_hbm, coarse_ref),
        (fine_hbm, fine_ref), (turn_hbm, turn_ref), (flip_hbm, flip_ref),
    )
    copies = [pltpu.make_async_copy(a, b, sems.at[n]) for n, (a, b) in enumerate(pairs)]
    for copy in copies:
        copy.start()
    turns = offset_tables(offsets_ref, lax.axis_index("facet"), width)
    for n in range(2):
        tables_ref[n] = turns["start"][n]
        tables_ref[2 + n] = turns["cell"][n]
    high, low, centre = turns["tile"], turns["inner"], turns["middle"]
    for tile in range(half // LANES):
        c, s = high[0][:, tile : tile + 1], high[1][:, tile : tile + 1]
        span = slice(tile * LANES, (tile + 1) * LANES)
        phase_ref[0, :, span] = c * low[0] - s * low[1]
        phase_ref[1, :, span] = s * low[0] + c * low[1]
    for copy in copies:
        copy.wait()

    def windowed(span):
        product = slab_ref[:, span].astype(jnp.float32) * window_ref[:, span]
        return product.astype(jnp.bfloat16)

    def stage_columns(tile, fine):
        span = slice(tile * STEP, (tile + 1) * STEP)
        slot = tile % 2
        if fine == 0:
            side_ref[0] = windowed(
                slice(half + tile * STEP, half + (tile + 1) * STEP)
            ).astype(jnp.float32)
            side_ref[1] = lax.dot_general(
                windowed(slice(half - (tile + 1) * STEP, half - tile * STEP)), flip_ref[...], NN,
                preferred_element_type=jnp.float32,
            )
        sides = []
        for n in range(2):
            re, im = side_ref[n, :columns], side_ref[n, columns:]
            if fine > 0:
                row = (2 * fine + n) * 2
                c, s = fine_ref[row : row + 1, span], fine_ref[row + 1 : row + 2, span]
                re, im = re * c + im * s, im * c - re * s
            sides.append((re, im))
        (re_p, im_p), (re_m, im_m) = sides
        upper = slice(2 * columns * fine, 2 * columns * fine + columns)
        lower = slice(2 * columns * fine + columns, 2 * columns * (fine + 1))
        wave_ref[slot, upper, :STEP] = (re_p + re_m).astype(jnp.bfloat16)
        wave_ref[slot, lower, :STEP] = (im_p + im_m).astype(jnp.bfloat16)
        wave_ref[slot, upper, STEP:] = (im_p - im_m).astype(jnp.bfloat16)
        wave_ref[slot, lower, STEP:] = (re_m - re_p).astype(jnp.bfloat16)

    def stage_rows(tile, s):
        span = slice(tile * STEP, (tile + 1) * STEP)
        where = slice(s * rows, (s + 1) * rows)
        cj, sj = coarse_ref[0, :, span], coarse_ref[1, :, span]
        co, so = phase_ref[0, s : s + 1, span], phase_ref[1, s : s + 1, span]
        turn_table_ref[tile % 2, where, :STEP] = (co * cj - so * sj).astype(jnp.bfloat16)
        turn_table_ref[tile % 2, where, STEP:] = (so * cj + co * sj).astype(jnp.bfloat16)

    cm, sm = turn_ref[0], turn_ref[1]
    scale = width ** (-0.5)
    sign = jnp.where(
        lax.broadcasted_iota(jnp.int32, (1, 2 * columns), 1) < columns, scale, -scale
    )

    def finish(s):
        co, so = centre[0][s : s + 1], centre[1][s : s + 1]
        c = (co * cm + so * sm) * scale
        d = (so * cm - co * sm) * sign
        blocks = []
        for fine in range(FINE):
            block = total_ref[s * rows : (s + 1) * rows, fine * LANES : (fine + 1) * LANES]
            blocks.append(block * c + pltpu.roll(block, columns, 1) * d)
        down = jnp.concatenate(blocks, 0).T
        per = out_ref.shape[2] // 2
        for layer in range(out_ref.shape[0]):
            first = layer * per
            out_ref[layer, s] = jnp.concatenate(
                [down[first : first + per], down[columns + first : columns + first + per]], 0
            ).astype(jnp.bfloat16)

    steps = half // STEP
    each = subgrids // BLOCKS
    for fine in range(FINE):
        stage_columns(0, fine)
    for s in range(subgrids):
        stage_rows(0, s)
    for tile in range(steps):
        for block in range(BLOCKS):
            where = slice(block * each * rows, (block + 1) * each * rows)
            part = lax.dot_general(
                turn_table_ref[tile % 2, where], wave_ref[tile % 2], NT,
                preferred_element_type=jnp.float32,
            )
            if tile == 0:
                total_ref[where] = part
            else:
                total_ref[where] += part
            if tile + 1 < steps:
                for fine in range(block * FINE // BLOCKS, (block + 1) * FINE // BLOCKS):
                    stage_columns(tile + 1, fine)
                for s in range(block * each, (block + 1) * each):
                    stage_rows(tile + 1, s)
            else:
                for s in range(block * each, (block + 1) * each):
                    finish(s)


def subgrid_kernel(
    recv_ref, kernel_ref, cos_ref, sin_ref, counts_hbm, part_ref, back_ref, out_ref,
    re_ref, im_ref, rows_ref, counts_ref, sem,
):
    layers, facets, tall, contrib = recv_ref.shape
    per = tall // 2
    cells = re_ref.shape[1]
    half = facets // 2
    copy = pltpu.make_async_copy(counts_hbm.at[:, lax.axis_index("layer")], counts_ref, sem)
    copy.start()
    for f in range(facets // 4):
        first, second, third, fourth = (
            recv_ref[:, n].astype(jnp.float32)
            for n in (f, f + half, facets - 1 - f, half - 1 - f)
        )
        for parity in range(2):
            span = slice(parity * cells // 2, (parity + 1) * cells // 2)
            near = first + second if parity == 0 else first - second
            far = third + fourth if parity == 0 else third - fourth
            both = jnp.concatenate([near + far, near - far], 0)
            wide = lax.dot_general(
                both.reshape(2 * layers * tall, contrib).astype(jnp.bfloat16),
                kernel_ref[:, span], NN, preferred_element_type=jnp.float32,
            ).reshape(2, layers, 2, per, cells // 2)
            even_re, even_im, odd_re, odd_im = (
                wide[a, :, b].reshape(layers * per, cells // 2) for a in range(2) for b in range(2)
            )
            c, s = cos_ref[f : f + 1, span], sin_ref[f : f + 1, span]
            re = even_re * c + odd_im * s
            im = even_im * c - odd_re * s
            if f == 0:
                re_ref[:, span] = re
                im_ref[:, span] = im
            else:
                re_ref[:, span] += re
                im_ref[:, span] += im
    copy.wait()
    held = counts_ref[...].astype(jnp.float32).reshape(layers, 2, per, cells // 2)
    counts = 0.0
    for n in range(2):
        counts = counts + lax.dot_general(
            held[:, n].reshape(layers * per, cells // 2).astype(jnp.bfloat16),
            part_ref[n * cells // 2 : (n + 1) * cells // 2], NN,
            preferred_element_type=jnp.float32,
        )
    weights = jnp.where(counts > 0, 1.0 / jnp.maximum(counts, 1.0), 0.0) * (
        (2 * facets) ** (-0.5)
    )
    re = jnp.sum((re_ref[...] * weights).reshape(layers, per, cells), axis=0)
    im = jnp.sum((im_ref[...] * weights).reshape(layers, per, cells), axis=0)
    for f in range(facets):
        c, s = cos_ref[f : f + 1, :], sin_ref[f : f + 1, :]
        turned = jnp.concatenate([re * c - im * s, im * c + re * s], 0)
        rows_ref[f * tall : (f + 1) * tall, :] = turned.astype(jnp.bfloat16)
    back = lax.dot_general(
        rows_ref[...], back_ref[...], NT, preferred_element_type=jnp.float32
    )
    out_ref[...] = (back * 0.5).astype(jnp.bfloat16).reshape(out_ref.shape)


def decode_kernel(
    recv_ref, window_ref, tables_ref, table_ref, out_ref, pr_ref, pi_ref
):
    subgrids = recv_ref.shape[0]
    per = recv_ref.shape[1] // 2
    width = out_ref.shape[2]
    for tile in range(width // LANES):
        c, s = tables_ref[0, :, tile : tile + 1], tables_ref[1, :, tile : tile + 1]
        span = slice(tile * LANES, (tile + 1) * LANES)
        pr_ref[:, span] = c * tables_ref[2] - s * tables_ref[3]
        pi_ref[:, span] = s * tables_ref[2] + c * tables_ref[3]
    rows = recv_ref[...].astype(jnp.float32)
    re, im = rows[:, :per], rows[:, per:]
    left_re = jnp.concatenate([re, im], 2).reshape(subgrids * per, 2 * CONTRIB).astype(jnp.bfloat16)
    left_im = jnp.concatenate([im, -re], 2).reshape(subgrids * per, 2 * CONTRIB).astype(jnp.bfloat16)
    scale = (subgrids * CONTRIB) ** (-0.5)
    for tile in range(width // 256):
        span = slice(tile * 256, (tile + 1) * 256)
        table = table_ref[:, span]
        zr = lax.dot_general(left_re, table, NN, preferred_element_type=jnp.float32)
        zi = lax.dot_general(left_im, table, NN, preferred_element_type=jnp.float32)
        out_re, out_im = None, None
        for s in range(subgrids):
            a = zr[s * per : (s + 1) * per]
            b = zi[s * per : (s + 1) * per]
            pr = pr_ref[s : s + 1, span]
            pi = pi_ref[s : s + 1, span]
            re_term = pr * a - pi * b
            im_term = pr * b + pi * a
            out_re = re_term if out_re is None else out_re + re_term
            out_im = im_term if out_im is None else out_im + im_term
        taper = window_ref[:, span] * scale
        out_ref[0, :, span] = out_re * taper
        out_ref[1, :, span] = out_im * taper


def params(mebibytes):
    return pltpu.CompilerParams(vmem_limit_bytes=mebibytes * 2**20)


def shards(slabs, window, density, offsets):
    layers = lax.axis_size("layer")
    facets = lax.axis_size("facet")
    columns, width = slabs.shape[2], slabs.shape[3]
    per = columns // layers
    sample_step = SUB // CONTRIB
    image_width = width * facets
    table = jnp.asarray(step_table(width, image_width, sample_step))
    folds = [jnp.asarray(part) for part in fold_tables(width, image_width, sample_step)]
    cells = np.concatenate([np.arange(0, SUB, 2), np.arange(1, SUB, 2)])
    spreading = np.ascontiguousarray(kernel_table(sample_step)[:, cells])
    parting = np.eye(SUB)[:, cells].astype(ml_dtypes.bfloat16)
    spread = jnp.asarray(spreading)
    order = np.arange(CONTRIB).reshape(CONTRIB // FINE, FINE).T.reshape(-1)
    spread_in = jnp.asarray(np.ascontiguousarray(spreading[order]))
    cos_u, sin_u = (
        jnp.asarray(np.ascontiguousarray(part[:, cells])) for part in centre_phases(facets)
    )

    window_row = window.reshape(1, width)

    whole = pl.BlockSpec(memory_space=pltpu.VMEM)
    counts = density.reshape(layers, per, 2, SUB // 2).transpose(0, 2, 1, 3)
    counts = counts.reshape(layers, 2 * per, SUB // 2).astype(jnp.bfloat16)
    counts = lax.all_gather(counts, "layer")
    anywhere = pl.BlockSpec(memory_space=pl.ANY)
    rows = facets * CONTRIB // FINE
    wide = 2 * columns * FINE
    half = width // 2
    outgoing, tables = pl.pallas_call(
        encode_kernel,
        out_shape=(
            jax.ShapeDtypeStruct((layers, facets, 2 * per, CONTRIB), jnp.bfloat16),
            jax.ShapeDtypeStruct((4, facets, LANES), jnp.float32),
        ),
        in_specs=[anywhere, anywhere, whole] + [anywhere] * 4,
        out_specs=(whole, whole),
        scratch_shapes=[
            pltpu.VMEM((2 * columns, width), jnp.bfloat16),
            pltpu.VMEM((1, width), jnp.float32),
            pltpu.VMEM((2, CONTRIB // FINE, half), jnp.float32),
            pltpu.VMEM((4 * FINE, half), jnp.float32),
            pltpu.VMEM((2, CONTRIB // FINE, LANES), jnp.float32),
            pltpu.VMEM((STEP, STEP), jnp.bfloat16),
            pltpu.VMEM((2, facets, half), jnp.float32),
            pltpu.VMEM((2, 2 * columns, STEP), jnp.float32),
            pltpu.VMEM((2, rows, 2 * STEP), jnp.bfloat16),
            pltpu.VMEM((2, wide, 2 * STEP), jnp.bfloat16),
            pltpu.VMEM((rows, wide), jnp.float32),
            pltpu.SemaphoreType.DMA((6,)),
        ],
        compiler_params=params(60),
        cost_estimate=pl.CostEstimate(
            flops=4 * rows * half * wide, bytes_accessed=4 * width * rows, transcendentals=0
        ),
        name="encode",
    )(slabs.reshape(2 * columns, width), window_row, offsets.reshape(1, facets), *folds)

    received = lax.all_to_all(
        outgoing.reshape(layers * facets, 2 * per, CONTRIB), ("layer", "facet"),
        split_axis=0, concat_axis=0, tiled=True,
    ).reshape(layers, facets, 2 * per, CONTRIB)

    back_out = pl.pallas_call(
        subgrid_kernel,
        out_shape=jax.ShapeDtypeStruct((facets, 2 * per, CONTRIB), jnp.bfloat16),
        in_specs=[whole] * 4 + [anywhere] + [whole] * 2,
        out_specs=whole,
        scratch_shapes=[
            pltpu.VMEM((columns, SUB), jnp.float32),
            pltpu.VMEM((columns, SUB), jnp.float32),
            pltpu.VMEM((facets * 2 * per, SUB), jnp.bfloat16),
            pltpu.VMEM((layers, 2 * per, SUB // 2), jnp.bfloat16),
            pltpu.SemaphoreType.DMA(()),
        ],
        compiler_params=params(48),
        name="subgrid",
    )(received, spread_in, cos_u, sin_u, counts, jnp.asarray(parting), spread)

    returned = lax.all_to_all(back_out, "facet", split_axis=0, concat_axis=0, tiled=True)

    return pl.pallas_call(
        decode_kernel,
        out_shape=jax.ShapeDtypeStruct((2, per, width), jnp.float32),
        in_specs=[whole] * 4,
        out_specs=whole,
        scratch_shapes=[pltpu.VMEM((facets, width), jnp.float32)] * 2,
        compiler_params=params(48),
        name="decode",
    )(returned, window_row, tables, table)


def solution(mesh):
    placed = (P("layer", None, None, "facet"), P("facet"), P("layer", None, "facet"), P())
    return jax.shard_map(
        shards, mesh=mesh, in_specs=placed, out_specs=P(None, "layer", "facet"), check_vma=False
    )
```

```python
import math

import jax
import jax.numpy as jnp
import ml_dtypes
import numpy as np
from jax import lax
from jax.experimental import pallas as pl
from jax.experimental.pallas import tpu as pltpu
from jax.sharding import PartitionSpec as P

CONTRIB = 128
SUB = 512
LANES = 128
FINE = 4
STEP = 256
BLOCKS = 2
SENT = 4

two_pi = 2.0 * math.pi
NT = (((1,), (1,)), ((), ()))
NN = (((1,), (0,)), ((), ()))


def step_table(facet_width, image_width, sample_step):
    j = np.arange(CONTRIB, dtype=np.int64)[:, None]
    cell = np.arange(facet_width, dtype=np.int64)[None, :] - facet_width // 2
    angle = np.mod(sample_step * j * cell, image_width) * (-2.0 * np.pi / image_width)
    return np.concatenate([np.cos(angle), np.sin(angle)], 0).astype(ml_dtypes.bfloat16)


def fold_tables(facet_width, image_width, sample_step):
    k = np.arange(facet_width // 2, dtype=np.int64)[None, :]
    j1 = np.arange(CONTRIB // FINE, dtype=np.int64)[:, None]
    j2 = np.arange(FINE, dtype=np.int64)[:, None]

    def parts(turns):
        angle = np.mod(turns, image_width) * (2.0 * np.pi / image_width)
        return np.stack([np.cos(angle), np.sin(angle)]).astype(np.float32)

    half_step = sample_step * FINE // 2
    coarse = parts(half_step * j1 * (2 * k + 1))
    fine = np.stack([parts(sample_step * j2 * k), parts(-sample_step * j2 * (k + 1))])
    fine = fine.transpose(2, 0, 1, 3).reshape(4 * FINE, facet_width // 2)
    turn = np.broadcast_to(parts(half_step * j1), (2, CONTRIB // FINE, LANES))
    flip = np.eye(STEP)[::-1].astype(ml_dtypes.bfloat16)
    return coarse, np.ascontiguousarray(fine), np.ascontiguousarray(turn), np.ascontiguousarray(flip)


def kernel_table(sample_step):
    spacing = np.arange(SUB)[None, :] - sample_step * np.arange(CONTRIB)[:, None]
    scaled = spacing / sample_step
    return (1.0 / (1.0 + scaled * scaled)).astype(ml_dtypes.bfloat16)


def centre_phases(facets):
    turns = np.mod(
        np.arange(SUB)[None, :] * (2 * np.arange(facets)[:, None] + 1), 2 * facets
    )
    angle = turns * (np.pi / facets)
    return np.cos(angle).astype(np.float32), np.sin(angle).astype(np.float32)


def offset_tables(offsets_ref, position, width):
    subgrids = offsets_ref.shape[1]
    image_width = width * subgrids
    down = lax.broadcasted_iota(jnp.int32, (subgrids, subgrids), 0)
    across = lax.broadcasted_iota(jnp.int32, (subgrids, subgrids), 1)
    column = jnp.sum(jnp.where(down == across, offsets_ref[...], 0), axis=1, keepdims=True)
    lane = lax.broadcasted_iota(jnp.int32, (subgrids, LANES), 1)

    def parts(product, modulus):
        whole = jnp.floor(product.astype(jnp.float32) * (1.0 / modulus)).astype(jnp.int32)
        angle = (product - whole * modulus).astype(jnp.float32) * (two_pi / modulus)
        return jnp.cos(angle), jnp.sin(angle)

    facet_turns = jnp.bitwise_and(column * position, subgrids - 1)
    return {
        "start": parts(column * (position * (width // LANES) + lane), image_width // LANES),
        "cell": parts(column * lane, image_width),
        "tile": parts(column * lane, image_width // LANES),
        "inner": parts(column * (2 * lane + 1), 2 * image_width),
        "middle": parts(
            column * (width - 1) + 2 * width * facet_turns + 0 * lane, 2 * image_width
        ),
    }


def encode_kernel(
    slab_hbm, window_hbm, offsets_ref, coarse_hbm, fine_hbm, turn_hbm, flip_hbm, out_hbm, cells_hbm,
    slab_ref, window_ref, coarse_ref, fine_ref, turn_ref, flip_ref,
    phase_ref, side_ref, turn_table_ref, wave_ref, total_ref,
    out_ref, cells_ref, sems, out_sems,
):
    columns = slab_ref.shape[0] // 2
    width = slab_ref.shape[1]
    half = width // 2
    subgrids = offsets_ref.shape[1]
    rows = CONTRIB // FINE
    pairs = (
        (slab_hbm, slab_ref), (window_hbm, window_ref), (coarse_hbm, coarse_ref),
        (fine_hbm, fine_ref), (turn_hbm, turn_ref), (flip_hbm, flip_ref),
    )
    copies = [pltpu.make_async_copy(a, b, sems.at[n]) for n, (a, b) in enumerate(pairs)]
    for copy in copies:
        copy.start()
    turns = offset_tables(offsets_ref, lax.axis_index("facet"), width)
    (cos_a, sin_a), (cos_b, sin_b) = turns["start"], turns["cell"]
    for tile in range(width // LANES):
        c, s = cos_a[:, tile : tile + 1], sin_a[:, tile : tile + 1]
        span = slice(tile * LANES, (tile + 1) * LANES)
        cells_ref[0, :, span] = c * cos_b - s * sin_b
        cells_ref[1, :, span] = s * cos_b + c * sin_b
    leaving = [pltpu.make_async_copy(cells_ref, cells_hbm, out_sems.at[subgrids // SENT])]
    leaving[0].start()
    high, low, centre = turns["tile"], turns["inner"], turns["middle"]
    for tile in range(half // LANES):
        c, s = high[0][:, tile : tile + 1], high[1][:, tile : tile + 1]
        span = slice(tile * LANES, (tile + 1) * LANES)
        phase_ref[0, :, span] = c * low[0] - s * low[1]
        phase_ref[1, :, span] = s * low[0] + c * low[1]
    for copy in copies:
        copy.wait()

    def windowed(span):
        product = slab_ref[:, span].astype(jnp.float32) * window_ref[:, span]
        return product.astype(jnp.bfloat16)

    def stage_columns(tile, fine):
        span = slice(tile * STEP, (tile + 1) * STEP)
        slot = tile % 2
        if fine == 0:
            side_ref[0] = windowed(
                slice(half + tile * STEP, half + (tile + 1) * STEP)
            ).astype(jnp.float32)
            side_ref[1] = lax.dot_general(
                windowed(slice(half - (tile + 1) * STEP, half - tile * STEP)), flip_ref[...], NN,
                preferred_element_type=jnp.float32,
            )
        sides = []
        for n in range(2):
            re, im = side_ref[n, :columns], side_ref[n, columns:]
            if fine > 0:
                row = (2 * fine + n) * 2
                c, s = fine_ref[row : row + 1, span], fine_ref[row + 1 : row + 2, span]
                re, im = re * c + im * s, im * c - re * s
            sides.append((re, im))
        (re_p, im_p), (re_m, im_m) = sides
        upper = slice(2 * columns * fine, 2 * columns * fine + columns)
        lower = slice(2 * columns * fine + columns, 2 * columns * (fine + 1))
        wave_ref[slot, upper, :STEP] = (re_p + re_m).astype(jnp.bfloat16)
        wave_ref[slot, lower, :STEP] = (im_p + im_m).astype(jnp.bfloat16)
        wave_ref[slot, upper, STEP:] = (im_p - im_m).astype(jnp.bfloat16)
        wave_ref[slot, lower, STEP:] = (re_m - re_p).astype(jnp.bfloat16)

    def stage_rows(tile, s):
        span = slice(tile * STEP, (tile + 1) * STEP)
        where = slice(s * rows, (s + 1) * rows)
        cj, sj = coarse_ref[0, :, span], coarse_ref[1, :, span]
        co, so = phase_ref[0, s : s + 1, span], phase_ref[1, s : s + 1, span]
        turn_table_ref[tile % 2, where, :STEP] = (co * cj - so * sj).astype(jnp.bfloat16)
        turn_table_ref[tile % 2, where, STEP:] = (so * cj + co * sj).astype(jnp.bfloat16)

    cm, sm = turn_ref[0], turn_ref[1]
    scale = width ** (-0.5)
    sign = jnp.where(
        lax.broadcasted_iota(jnp.int32, (1, 2 * columns), 1) < columns, scale, -scale
    )

    def finish(s):
        co, so = centre[0][s : s + 1], centre[1][s : s + 1]
        c = (co * cm + so * sm) * scale
        d = (so * cm - co * sm) * sign
        blocks = []
        for fine in range(FINE):
            block = total_ref[s * rows : (s + 1) * rows, fine * LANES : (fine + 1) * LANES]
            blocks.append(block * c + pltpu.roll(block, columns, 1) * d)
        out_ref[s] = jnp.concatenate(blocks, 0).astype(jnp.bfloat16).T

    steps = half // STEP
    each = subgrids // BLOCKS
    for fine in range(FINE):
        stage_columns(0, fine)
    for s in range(subgrids):
        stage_rows(0, s)
    for tile in range(steps):
        for block in range(BLOCKS):
            where = slice(block * each * rows, (block + 1) * each * rows)
            part = lax.dot_general(
                turn_table_ref[tile % 2, where], wave_ref[tile % 2], NT,
                preferred_element_type=jnp.float32,
            )
            if tile == 0:
                total_ref[where] = part
            else:
                total_ref[where] += part
            if tile + 1 < steps:
                for fine in range(block * FINE // BLOCKS, (block + 1) * FINE // BLOCKS):
                    stage_columns(tile + 1, fine)
                for s in range(block * each, (block + 1) * each):
                    stage_rows(tile + 1, s)
            else:
                for s in range(block * each, (block + 1) * each):
                    finish(s)
                    if s % SENT == SENT - 1:
                        done = slice(s + 1 - SENT, s + 1)
                        copy = pltpu.make_async_copy(
                            out_ref.at[done], out_hbm.at[done], out_sems.at[s // SENT]
                        )
                        copy.start()
                        leaving.append(copy)
    for copy in leaving:
        copy.wait()


def grid_kernel(
    recv_ref, kernel_ref, cos_ref, sin_ref, counts_ref, part_ref, out_ref, re_ref, im_ref
):
    facets = recv_ref.shape[0]
    columns = recv_ref.shape[1] // 2
    cells = re_ref.shape[1]
    half = facets // 2
    re_ref[...] = jnp.zeros_like(re_ref)
    im_ref[...] = jnp.zeros_like(im_ref)

    for f in range(facets // 4):
        first, second, third, fourth = (
            recv_ref[n].astype(jnp.float32) for n in (f, f + half, facets - 1 - f, half - 1 - f)
        )
        for parity in range(2):
            span = slice(parity * cells // 2, (parity + 1) * cells // 2)
            near = first + second if parity == 0 else first - second
            far = third + fourth if parity == 0 else third - fourth
            both = jnp.concatenate([near + far, near - far], 0).astype(jnp.bfloat16)
            wide = lax.dot_general(
                both, kernel_ref[:, span], NN, preferred_element_type=jnp.float32
            )
            even_re, even_im = wide[:columns], wide[columns : 2 * columns]
            odd_re, odd_im = wide[2 * columns : 3 * columns], wide[3 * columns :]
            c, s = cos_ref[f : f + 1, span], sin_ref[f : f + 1, span]
            re_ref[:, span] += even_re * c + odd_im * s
            im_ref[:, span] += even_im * c - odd_re * s

    counts = lax.dot_general(
        counts_ref[...].astype(jnp.float32).astype(jnp.bfloat16), part_ref[...], NN,
        preferred_element_type=jnp.float32,
    )
    weights = jnp.where(counts > 0, 1.0 / jnp.maximum(counts, 1.0), 0.0) * (
        (2 * facets) ** (-0.5)
    )
    re = re_ref[...] * weights
    im = im_ref[...] * weights
    per = out_ref.shape[1] // 2
    for layer in range(out_ref.shape[0]):
        span = slice(layer * per, (layer + 1) * per)
        out_ref[layer] = jnp.concatenate([re[span], im[span]], 0).astype(jnp.bfloat16)


def back_kernel(recv_ref, kernel_ref, cos_ref, sin_ref, out_ref, rows_ref):
    layers = recv_ref.shape[0]
    facets = out_ref.shape[0]
    total = recv_ref[0].astype(jnp.float32)
    for layer in range(1, layers):
        total = total + recv_ref[layer].astype(jnp.float32)
    per = total.shape[0] // 2
    re, im = total[:per], total[per:]
    for f in range(facets):
        c = cos_ref[f : f + 1, :]
        s = sin_ref[f : f + 1, :]
        turned = jnp.concatenate([re * c - im * s, im * c + re * s], 0)
        rows_ref[f * 2 * per : (f + 1) * 2 * per, :] = turned.astype(jnp.bfloat16)
    back = lax.dot_general(
        rows_ref[...], kernel_ref[...], NT, preferred_element_type=jnp.float32
    )
    out_ref[...] = (back * 0.5).astype(jnp.bfloat16).reshape(out_ref.shape)


def decode_kernel(
    recv_ref, window_ref, phases_ref, table_ref, out_ref
):
    subgrids = recv_ref.shape[0]
    per = recv_ref.shape[1] // 2
    width = out_ref.shape[2]
    rows = recv_ref[...].astype(jnp.float32)
    re, im = rows[:, :per], rows[:, per:]
    left_re = jnp.concatenate([re, im], 2).reshape(subgrids * per, 2 * CONTRIB).astype(jnp.bfloat16)
    left_im = jnp.concatenate([im, -re], 2).reshape(subgrids * per, 2 * CONTRIB).astype(jnp.bfloat16)
    scale = (subgrids * CONTRIB) ** (-0.5)
    for tile in range(width // 256):
        span = slice(tile * 256, (tile + 1) * 256)
        table = table_ref[:, span]
        zr = lax.dot_general(left_re, table, NN, preferred_element_type=jnp.float32)
        zi = lax.dot_general(left_im, table, NN, preferred_element_type=jnp.float32)
        out_re, out_im = None, None
        for s in range(subgrids):
            a = zr[s * per : (s + 1) * per]
            b = zi[s * per : (s + 1) * per]
            pr = phases_ref[0, s : s + 1, span]
            pi = phases_ref[1, s : s + 1, span]
            re_term = pr * a - pi * b
            im_term = pr * b + pi * a
            out_re = re_term if out_re is None else out_re + re_term
            out_im = im_term if out_im is None else out_im + im_term
        taper = window_ref[:, span] * scale
        out_ref[0, :, span] = out_re * taper
        out_ref[1, :, span] = out_im * taper


def params(mebibytes):
    return pltpu.CompilerParams(vmem_limit_bytes=mebibytes * 2**20)


def shards(slabs, window, density, offsets):
    layers = lax.axis_size("layer")
    facets = lax.axis_size("facet")
    columns, width = slabs.shape[2], slabs.shape[3]
    per = columns // layers
    sample_step = SUB // CONTRIB
    image_width = width * facets
    table = jnp.asarray(step_table(width, image_width, sample_step))
    folds = [jnp.asarray(part) for part in fold_tables(width, image_width, sample_step)]
    cells = np.concatenate([np.arange(0, SUB, 2), np.arange(1, SUB, 2)])
    spreading = np.ascontiguousarray(kernel_table(sample_step)[:, cells])
    parting = np.eye(SUB)[:, cells].astype(ml_dtypes.bfloat16)
    spread = jnp.asarray(spreading)
    order = np.arange(CONTRIB).reshape(CONTRIB // FINE, FINE).T.reshape(-1)
    spread_in = jnp.asarray(np.ascontiguousarray(spreading[order]))
    cos_u, sin_u = (
        jnp.asarray(np.ascontiguousarray(part[:, cells])) for part in centre_phases(facets)
    )

    window_row = window.reshape(1, width)

    whole = pl.BlockSpec(memory_space=pltpu.VMEM)
    anywhere = pl.BlockSpec(memory_space=pl.ANY)
    rows = facets * CONTRIB // FINE
    wide = 2 * columns * FINE
    half = width // 2
    outgoing, cell_phases = pl.pallas_call(
        encode_kernel,
        out_shape=(
            jax.ShapeDtypeStruct((facets, 2 * columns, CONTRIB), jnp.bfloat16),
            jax.ShapeDtypeStruct((2, facets, width), jnp.float32),
        ),
        in_specs=[anywhere, anywhere, whole] + [anywhere] * 4,
        out_specs=(anywhere, anywhere),
        scratch_shapes=[
            pltpu.VMEM((2 * columns, width), jnp.bfloat16),
            pltpu.VMEM((1, width), jnp.float32),
            pltpu.VMEM((2, CONTRIB // FINE, half), jnp.float32),
            pltpu.VMEM((4 * FINE, half), jnp.float32),
            pltpu.VMEM((2, CONTRIB // FINE, LANES), jnp.float32),
            pltpu.VMEM((STEP, STEP), jnp.bfloat16),
            pltpu.VMEM((2, facets, half), jnp.float32),
            pltpu.VMEM((2, 2 * columns, STEP), jnp.float32),
            pltpu.VMEM((2, rows, 2 * STEP), jnp.bfloat16),
            pltpu.VMEM((2, wide, 2 * STEP), jnp.bfloat16),
            pltpu.VMEM((rows, wide), jnp.float32),
            pltpu.VMEM((facets, 2 * columns, CONTRIB), jnp.bfloat16),
            pltpu.VMEM((2, facets, width), jnp.float32),
            pltpu.SemaphoreType.DMA((6,)),
            pltpu.SemaphoreType.DMA((facets // SENT + 1,)),
        ],
        compiler_params=params(60),
        name="encode",
    )(slabs.reshape(2 * columns, width), window_row, offsets.reshape(1, facets), *folds)

    received = lax.all_to_all(outgoing, "facet", split_axis=0, concat_axis=0, tiled=True)

    gridded = pl.pallas_call(
        grid_kernel,
        out_shape=jax.ShapeDtypeStruct((layers, 2 * per, SUB), jnp.bfloat16),
        in_specs=[whole] * 6,
        out_specs=whole,
        scratch_shapes=[pltpu.VMEM((columns, SUB), jnp.float32)] * 2,
        compiler_params=params(48),
        name="subgrid",
    )(received, spread_in, cos_u, sin_u, density[0], jnp.asarray(parting))

    by_layer = lax.all_to_all(gridded, "layer", split_axis=0, concat_axis=0, tiled=True)

    back_out = pl.pallas_call(
        back_kernel,
        out_shape=jax.ShapeDtypeStruct((facets, 2 * per, CONTRIB), jnp.bfloat16),
        in_specs=[whole] * 4,
        out_specs=whole,
        scratch_shapes=[pltpu.VMEM((facets * 2 * per, SUB), jnp.bfloat16)],
        compiler_params=params(48),
        name="back",
    )(by_layer, spread, cos_u, sin_u)

    returned = lax.all_to_all(back_out, "facet", split_axis=0, concat_axis=0, tiled=True)

    return pl.pallas_call(
        decode_kernel,
        out_shape=jax.ShapeDtypeStruct((2, per, width), jnp.float32),
        in_specs=[whole] * 4,
        out_specs=whole,
        compiler_params=params(48),
        name="decode",
    )(returned, window_row, cell_phases, table)


def solution(mesh):
    placed = (P("layer", None, None, "facet"), P("facet"), P("layer", None, "facet"), P())
    return jax.shard_map(
        shards, mesh=mesh, in_specs=placed, out_specs=P(None, "layer", "facet"), check_vma=False
    )
```

```python
import math

import jax
import jax.numpy as jnp
import ml_dtypes
import numpy as np
from jax import lax
from jax.experimental import pallas as pl
from jax.experimental.pallas import tpu as pltpu
from jax.sharding import PartitionSpec as P

CONTRIB = 128
SUB = 512
LANES = 128
FINE = 4
STEP = 256
BLOCKS = 2
SENT = 4

two_pi = 2.0 * math.pi
NT = (((1,), (1,)), ((), ()))
NN = (((1,), (0,)), ((), ()))


def step_table(facet_width, image_width, sample_step):
    j = np.arange(CONTRIB, dtype=np.int64)[:, None]
    cell = np.arange(facet_width, dtype=np.int64)[None, :] - facet_width // 2
    angle = np.mod(sample_step * j * cell, image_width) * (-2.0 * np.pi / image_width)
    return np.concatenate([np.cos(angle), np.sin(angle)], 0).astype(ml_dtypes.bfloat16)


def fold_tables(facet_width, image_width, sample_step):
    k = np.arange(facet_width // 2, dtype=np.int64)[None, :]
    j1 = np.arange(CONTRIB // FINE, dtype=np.int64)[:, None]
    j2 = np.arange(FINE, dtype=np.int64)[:, None]

    def parts(turns):
        angle = np.mod(turns, image_width) * (2.0 * np.pi / image_width)
        return np.stack([np.cos(angle), np.sin(angle)]).astype(np.float32)

    half_step = sample_step * FINE // 2
    coarse = parts(half_step * j1 * (2 * k + 1))
    fine = np.stack([parts(sample_step * j2 * k), parts(-sample_step * j2 * (k + 1))])
    fine = fine.transpose(2, 0, 1, 3).reshape(4 * FINE, facet_width // 2)
    turn = np.broadcast_to(parts(half_step * j1), (2, CONTRIB // FINE, LANES))
    flip = np.eye(STEP)[::-1].astype(ml_dtypes.bfloat16)
    return coarse, np.ascontiguousarray(fine), np.ascontiguousarray(turn), np.ascontiguousarray(flip)


def kernel_table(sample_step):
    spacing = np.arange(SUB)[None, :] - sample_step * np.arange(CONTRIB)[:, None]
    scaled = spacing / sample_step
    return (1.0 / (1.0 + scaled * scaled)).astype(ml_dtypes.bfloat16)


def centre_phases(facets):
    turns = np.mod(
        np.arange(SUB)[None, :] * (2 * np.arange(facets)[:, None] + 1), 2 * facets
    )
    angle = turns * (np.pi / facets)
    return np.cos(angle).astype(np.float32), np.sin(angle).astype(np.float32)


def offset_tables(offsets_ref, position, width):
    subgrids = offsets_ref.shape[1]
    image_width = width * subgrids
    down = lax.broadcasted_iota(jnp.int32, (subgrids, subgrids), 0)
    across = lax.broadcasted_iota(jnp.int32, (subgrids, subgrids), 1)
    column = jnp.sum(jnp.where(down == across, offsets_ref[...], 0), axis=1, keepdims=True)
    lane = lax.broadcasted_iota(jnp.int32, (subgrids, LANES), 1)

    def parts(product, modulus):
        whole = jnp.floor(product.astype(jnp.float32) * (1.0 / modulus)).astype(jnp.int32)
        angle = (product - whole * modulus).astype(jnp.float32) * (two_pi / modulus)
        return jnp.cos(angle), jnp.sin(angle)

    facet_turns = jnp.bitwise_and(column * position, subgrids - 1)
    return {
        "start": parts(column * (position * (width // LANES) + lane), image_width // LANES),
        "cell": parts(column * lane, image_width),
        "tile": parts(column * lane, image_width // LANES),
        "inner": parts(column * (2 * lane + 1), 2 * image_width),
        "middle": parts(
            column * (width - 1) + 2 * width * facet_turns + 0 * lane, 2 * image_width
        ),
    }


def encode_kernel(
    slab_hbm, window_hbm, offsets_ref, coarse_hbm, fine_hbm, turn_hbm, flip_hbm, out_hbm, cells_hbm,
    slab_ref, window_ref, coarse_ref, fine_ref, turn_ref, flip_ref,
    phase_ref, side_ref, turn_table_ref, wave_ref, total_ref,
    out_ref, cells_ref, sems, out_sems,
):
    columns = slab_ref.shape[0] // 2
    width = slab_ref.shape[1]
    half = width // 2
    subgrids = offsets_ref.shape[1]
    rows = CONTRIB // FINE
    pairs = (
        (slab_hbm, slab_ref), (window_hbm, window_ref), (coarse_hbm, coarse_ref),
        (fine_hbm, fine_ref), (turn_hbm, turn_ref), (flip_hbm, flip_ref),
    )
    copies = [pltpu.make_async_copy(a, b, sems.at[n]) for n, (a, b) in enumerate(pairs)]
    for copy in copies:
        copy.start()
    turns = offset_tables(offsets_ref, lax.axis_index("facet"), width)
    (cos_a, sin_a), (cos_b, sin_b) = turns["start"], turns["cell"]
    for tile in range(width // LANES):
        c, s = cos_a[:, tile : tile + 1], sin_a[:, tile : tile + 1]
        span = slice(tile * LANES, (tile + 1) * LANES)
        cells_ref[0, :, span] = c * cos_b - s * sin_b
        cells_ref[1, :, span] = s * cos_b + c * sin_b
    leaving = [pltpu.make_async_copy(cells_ref, cells_hbm, out_sems.at[subgrids // SENT])]
    leaving[0].start()
    high, low, centre = turns["tile"], turns["inner"], turns["middle"]
    for tile in range(half // LANES):
        c, s = high[0][:, tile : tile + 1], high[1][:, tile : tile + 1]
        span = slice(tile * LANES, (tile + 1) * LANES)
        phase_ref[0, :, span] = c * low[0] - s * low[1]
        phase_ref[1, :, span] = s * low[0] + c * low[1]
    for copy in copies:
        copy.wait()

    def windowed(span):
        product = slab_ref[:, span].astype(jnp.float32) * window_ref[:, span]
        return product.astype(jnp.bfloat16)

    def stage_columns(tile, fine):
        span = slice(tile * STEP, (tile + 1) * STEP)
        slot = tile % 2
        if fine == 0:
            side_ref[0] = windowed(
                slice(half + tile * STEP, half + (tile + 1) * STEP)
            ).astype(jnp.float32)
            side_ref[1] = lax.dot_general(
                windowed(slice(half - (tile + 1) * STEP, half - tile * STEP)), flip_ref[...], NN,
                preferred_element_type=jnp.float32,
            )
        sides = []
        for n in range(2):
            re, im = side_ref[n, :columns], side_ref[n, columns:]
            if fine > 0:
                row = (2 * fine + n) * 2
                c, s = fine_ref[row : row + 1, span], fine_ref[row + 1 : row + 2, span]
                re, im = re * c + im * s, im * c - re * s
            sides.append((re, im))
        (re_p, im_p), (re_m, im_m) = sides
        upper = slice(2 * columns * fine, 2 * columns * fine + columns)
        lower = slice(2 * columns * fine + columns, 2 * columns * (fine + 1))
        wave_ref[slot, upper, :STEP] = (re_p + re_m).astype(jnp.bfloat16)
        wave_ref[slot, lower, :STEP] = (im_p + im_m).astype(jnp.bfloat16)
        wave_ref[slot, upper, STEP:] = (im_p - im_m).astype(jnp.bfloat16)
        wave_ref[slot, lower, STEP:] = (re_m - re_p).astype(jnp.bfloat16)

    def stage_rows(tile, s):
        span = slice(tile * STEP, (tile + 1) * STEP)
        where = slice(s * rows, (s + 1) * rows)
        cj, sj = coarse_ref[0, :, span], coarse_ref[1, :, span]
        co, so = phase_ref[0, s : s + 1, span], phase_ref[1, s : s + 1, span]
        turn_table_ref[tile % 2, where, :STEP] = (co * cj - so * sj).astype(jnp.bfloat16)
        turn_table_ref[tile % 2, where, STEP:] = (so * cj + co * sj).astype(jnp.bfloat16)

    cm, sm = turn_ref[0], turn_ref[1]
    scale = width ** (-0.5)
    sign = jnp.where(
        lax.broadcasted_iota(jnp.int32, (1, 2 * columns), 1) < columns, scale, -scale
    )

    def finish(s):
        co, so = centre[0][s : s + 1], centre[1][s : s + 1]
        c = (co * cm + so * sm) * scale
        d = (so * cm - co * sm) * sign
        blocks = []
        for fine in range(FINE):
            block = total_ref[s * rows : (s + 1) * rows, fine * LANES : (fine + 1) * LANES]
            blocks.append(block * c + pltpu.roll(block, columns, 1) * d)
        out_ref[s] = jnp.concatenate(blocks, 0).astype(jnp.bfloat16).T

    steps = half // STEP
    each = subgrids // BLOCKS
    for fine in range(FINE):
        stage_columns(0, fine)
    for s in range(subgrids):
        stage_rows(0, s)
    for tile in range(steps):
        for block in range(BLOCKS):
            where = slice(block * each * rows, (block + 1) * each * rows)
            part = lax.dot_general(
                turn_table_ref[tile % 2, where], wave_ref[tile % 2], NT,
                preferred_element_type=jnp.float32,
            )
            if tile == 0:
                total_ref[where] = part
            else:
                total_ref[where] += part
            if tile + 1 < steps:
                for fine in range(block * FINE // BLOCKS, (block + 1) * FINE // BLOCKS):
                    stage_columns(tile + 1, fine)
                for s in range(block * each, (block + 1) * each):
                    stage_rows(tile + 1, s)
            else:
                for s in range(block * each, (block + 1) * each):
                    finish(s)
                    if s % SENT == SENT - 1:
                        done = slice(s + 1 - SENT, s + 1)
                        copy = pltpu.make_async_copy(
                            out_ref.at[done], out_hbm.at[done], out_sems.at[s // SENT]
                        )
                        copy.start()
                        leaving.append(copy)
    for copy in leaving:
        copy.wait()


def grid_kernel(
    recv_ref, kernel_ref, cos_ref, sin_ref, counts_ref, part_ref, out_ref, re_ref, im_ref
):
    facets = recv_ref.shape[0]
    columns = recv_ref.shape[1] // 2
    cells = re_ref.shape[1]
    half = facets // 2
    re_ref[...] = jnp.zeros_like(re_ref)
    im_ref[...] = jnp.zeros_like(im_ref)

    for f in range(facets // 4):
        first, second, third, fourth = (
            recv_ref[n].astype(jnp.float32) for n in (f, f + half, facets - 1 - f, half - 1 - f)
        )
        for parity in range(2):
            span = slice(parity * cells // 2, (parity + 1) * cells // 2)
            near = first + second if parity == 0 else first - second
            far = third + fourth if parity == 0 else third - fourth
            both = jnp.concatenate([near + far, near - far], 0).astype(jnp.bfloat16)
            wide = lax.dot_general(
                both, kernel_ref[:, span], NN, preferred_element_type=jnp.float32
            )
            even_re, even_im = wide[:columns], wide[columns : 2 * columns]
            odd_re, odd_im = wide[2 * columns : 3 * columns], wide[3 * columns :]
            c, s = cos_ref[f : f + 1, span], sin_ref[f : f + 1, span]
            re_ref[:, span] += even_re * c + odd_im * s
            im_ref[:, span] += even_im * c - odd_re * s

    counts = lax.dot_general(
        counts_ref[...].astype(jnp.float32).astype(jnp.bfloat16), part_ref[...], NN,
        preferred_element_type=jnp.float32,
    )
    weights = jnp.where(counts > 0, 1.0 / jnp.maximum(counts, 1.0), 0.0) * (
        (2 * facets) ** (-0.5)
    )
    re = re_ref[...] * weights
    im = im_ref[...] * weights
    per = out_ref.shape[1] // 2
    for layer in range(out_ref.shape[0]):
        span = slice(layer * per, (layer + 1) * per)
        out_ref[layer] = jnp.concatenate([re[span], im[span]], 0).astype(jnp.bfloat16)


def back_kernel(recv_ref, kernel_ref, cos_ref, sin_ref, out_ref, rows_ref):
    layers = recv_ref.shape[0]
    facets = out_ref.shape[0]
    total = recv_ref[0].astype(jnp.float32)
    for layer in range(1, layers):
        total = total + recv_ref[layer].astype(jnp.float32)
    per = total.shape[0] // 2
    re, im = total[:per], total[per:]
    for f in range(facets):
        c = cos_ref[f : f + 1, :]
        s = sin_ref[f : f + 1, :]
        turned = jnp.concatenate([re * c - im * s, im * c + re * s], 0)
        rows_ref[f * 2 * per : (f + 1) * 2 * per, :] = turned.astype(jnp.bfloat16)
    back = lax.dot_general(
        rows_ref[...], kernel_ref[...], NT, preferred_element_type=jnp.float32
    )
    out_ref[...] = (back * 0.5).astype(jnp.bfloat16).reshape(out_ref.shape)


def decode_kernel(
    recv_ref, window_ref, phases_ref, table_ref, out_ref
):
    subgrids = recv_ref.shape[0]
    per = recv_ref.shape[1] // 2
    width = out_ref.shape[2]
    rows = recv_ref[...].astype(jnp.float32)
    re, im = rows[:, :per], rows[:, per:]
    left_re = jnp.concatenate([re, im], 2).reshape(subgrids * per, 2 * CONTRIB).astype(jnp.bfloat16)
    left_im = jnp.concatenate([im, -re], 2).reshape(subgrids * per, 2 * CONTRIB).astype(jnp.bfloat16)
    scale = (subgrids * CONTRIB) ** (-0.5)
    for tile in range(width // 256):
        span = slice(tile * 256, (tile + 1) * 256)
        table = table_ref[:, span]
        zr = lax.dot_general(left_re, table, NN, preferred_element_type=jnp.float32)
        zi = lax.dot_general(left_im, table, NN, preferred_element_type=jnp.float32)
        out_re, out_im = None, None
        for s in range(subgrids):
            a = zr[s * per : (s + 1) * per]
            b = zi[s * per : (s + 1) * per]
            pr = phases_ref[0, s : s + 1, span]
            pi = phases_ref[1, s : s + 1, span]
            re_term = pr * a - pi * b
            im_term = pr * b + pi * a
            out_re = re_term if out_re is None else out_re + re_term
            out_im = im_term if out_im is None else out_im + im_term
        taper = window_ref[:, span] * scale
        out_ref[0, :, span] = out_re * taper
        out_ref[1, :, span] = out_im * taper


def params(mebibytes):
    return pltpu.CompilerParams(vmem_limit_bytes=mebibytes * 2**20)


def shards(slabs, window, density, offsets):
    layers = lax.axis_size("layer")
    facets = lax.axis_size("facet")
    columns, width = slabs.shape[2], slabs.shape[3]
    per = columns // layers
    sample_step = SUB // CONTRIB
    image_width = width * facets
    table = jnp.asarray(step_table(width, image_width, sample_step))
    folds = [jnp.asarray(part) for part in fold_tables(width, image_width, sample_step)]
    cells = np.concatenate([np.arange(0, SUB, 2), np.arange(1, SUB, 2)])
    spreading = np.ascontiguousarray(kernel_table(sample_step)[:, cells])
    parting = np.eye(SUB)[:, cells].astype(ml_dtypes.bfloat16)
    spread = jnp.asarray(spreading)
    order = np.arange(CONTRIB).reshape(CONTRIB // FINE, FINE).T.reshape(-1)
    spread_in = jnp.asarray(np.ascontiguousarray(spreading[order]))
    cos_u, sin_u = (
        jnp.asarray(np.ascontiguousarray(part[:, cells])) for part in centre_phases(facets)
    )

    window_row = window.reshape(1, width)

    whole = pl.BlockSpec(memory_space=pltpu.VMEM)
    anywhere = pl.BlockSpec(memory_space=pl.ANY)
    rows = facets * CONTRIB // FINE
    wide = 2 * columns * FINE
    half = width // 2
    outgoing, cell_phases = pl.pallas_call(
        encode_kernel,
        out_shape=(
            jax.ShapeDtypeStruct((facets, 2 * columns, CONTRIB), jnp.bfloat16),
            jax.ShapeDtypeStruct((2, facets, width), jnp.float32),
        ),
        in_specs=[anywhere, anywhere, whole] + [anywhere] * 4,
        out_specs=(anywhere, anywhere),
        scratch_shapes=[
            pltpu.VMEM((2 * columns, width), jnp.bfloat16),
            pltpu.VMEM((1, width), jnp.float32),
            pltpu.VMEM((2, CONTRIB // FINE, half), jnp.float32),
            pltpu.VMEM((4 * FINE, half), jnp.float32),
            pltpu.VMEM((2, CONTRIB // FINE, LANES), jnp.float32),
            pltpu.VMEM((STEP, STEP), jnp.bfloat16),
            pltpu.VMEM((2, facets, half), jnp.float32),
            pltpu.VMEM((2, 2 * columns, STEP), jnp.float32),
            pltpu.VMEM((2, rows, 2 * STEP), jnp.bfloat16),
            pltpu.VMEM((2, wide, 2 * STEP), jnp.bfloat16),
            pltpu.VMEM((rows, wide), jnp.float32),
            pltpu.VMEM((facets, 2 * columns, CONTRIB), jnp.bfloat16),
            pltpu.VMEM((2, facets, width), jnp.float32),
            pltpu.SemaphoreType.DMA((6,)),
            pltpu.SemaphoreType.DMA((facets // SENT + 1,)),
        ],
        compiler_params=params(24),
        name="encode",
    )(slabs.reshape(2 * columns, width), window_row, offsets.reshape(1, facets), *folds)

    received = lax.all_to_all(outgoing, "facet", split_axis=0, concat_axis=0, tiled=True)

    gridded = pl.pallas_call(
        grid_kernel,
        out_shape=jax.ShapeDtypeStruct((layers, 2 * per, SUB), jnp.bfloat16),
        in_specs=[whole] * 6,
        out_specs=whole,
        scratch_shapes=[pltpu.VMEM((columns, SUB), jnp.float32)] * 2,
        compiler_params=params(48),
        name="subgrid",
    )(received, spread_in, cos_u, sin_u, density[0], jnp.asarray(parting))

    by_layer = lax.all_to_all(gridded, "layer", split_axis=0, concat_axis=0, tiled=True)

    back_out = pl.pallas_call(
        back_kernel,
        out_shape=jax.ShapeDtypeStruct((facets, 2 * per, CONTRIB), jnp.bfloat16),
        in_specs=[whole] * 4,
        out_specs=whole,
        scratch_shapes=[pltpu.VMEM((facets * 2 * per, SUB), jnp.bfloat16)],
        compiler_params=params(48),
        name="back",
    )(by_layer, spread, cos_u, sin_u)

    returned = lax.all_to_all(back_out, "facet", split_axis=0, concat_axis=0, tiled=True)

    return pl.pallas_call(
        decode_kernel,
        out_shape=jax.ShapeDtypeStruct((2, per, width), jnp.float32),
        in_specs=[whole] * 4,
        out_specs=whole,
        compiler_params=params(48),
        name="decode",
    )(returned, window_row, cell_phases, table)


def solution(mesh):
    placed = (P("layer", None, None, "facet"), P("facet"), P("layer", None, "facet"), P())
    return jax.shard_map(
        shards, mesh=mesh, in_specs=placed, out_specs=P(None, "layer", "facet"), check_vma=False
    )
```

```python
import math

import jax
import jax.numpy as jnp
import ml_dtypes
import numpy as np
from jax import lax
from jax.experimental import pallas as pl
from jax.experimental.pallas import tpu as pltpu
from jax.sharding import PartitionSpec as P

CONTRIB = 128
SUB = 512
LANES = 128
FINE = 4
STEP = 256
BLOCKS = 2
SENT = 4

two_pi = 2.0 * math.pi
NT = (((1,), (1,)), ((), ()))
NN = (((1,), (0,)), ((), ()))


def step_table(facet_width, image_width, sample_step):
    j = np.arange(CONTRIB, dtype=np.int64)[:, None]
    cell = np.arange(facet_width, dtype=np.int64)[None, :] - facet_width // 2
    angle = np.mod(sample_step * j * cell, image_width) * (-2.0 * np.pi / image_width)
    return np.concatenate([np.cos(angle), np.sin(angle)], 0).astype(ml_dtypes.bfloat16)


def fold_tables(facet_width, image_width, sample_step):
    k = np.arange(facet_width // 2, dtype=np.int64)[None, :]
    j1 = np.arange(CONTRIB // FINE, dtype=np.int64)[:, None]
    j2 = np.arange(FINE, dtype=np.int64)[:, None]

    def parts(turns):
        angle = np.mod(turns, image_width) * (2.0 * np.pi / image_width)
        return np.stack([np.cos(angle), np.sin(angle)]).astype(np.float32)

    half_step = sample_step * FINE // 2
    coarse = parts(half_step * j1 * (2 * k + 1))
    fine = np.stack([parts(sample_step * j2 * k), parts(-sample_step * j2 * (k + 1))])
    fine = fine.transpose(2, 0, 1, 3).reshape(4 * FINE, facet_width // 2)
    turn = np.broadcast_to(parts(half_step * j1), (2, CONTRIB // FINE, LANES))
    flip = np.eye(STEP)[::-1].astype(ml_dtypes.bfloat16)
    return coarse, np.ascontiguousarray(fine), np.ascontiguousarray(turn), np.ascontiguousarray(flip)


def kernel_table(sample_step):
    spacing = np.arange(SUB)[None, :] - sample_step * np.arange(CONTRIB)[:, None]
    scaled = spacing / sample_step
    return (1.0 / (1.0 + scaled * scaled)).astype(ml_dtypes.bfloat16)


def centre_phases(facets):
    turns = np.mod(
        np.arange(SUB)[None, :] * (2 * np.arange(facets)[:, None] + 1), 2 * facets
    )
    angle = turns * (np.pi / facets)
    return np.cos(angle).astype(np.float32), np.sin(angle).astype(np.float32)


def offset_tables(offsets_ref, position, width):
    subgrids = offsets_ref.shape[1]
    image_width = width * subgrids
    down = lax.broadcasted_iota(jnp.int32, (subgrids, subgrids), 0)
    across = lax.broadcasted_iota(jnp.int32, (subgrids, subgrids), 1)
    column = jnp.sum(jnp.where(down == across, offsets_ref[...], 0), axis=1, keepdims=True)
    lane = lax.broadcasted_iota(jnp.int32, (subgrids, LANES), 1)

    def parts(product, modulus):
        whole = jnp.floor(product.astype(jnp.float32) * (1.0 / modulus)).astype(jnp.int32)
        angle = (product - whole * modulus).astype(jnp.float32) * (two_pi / modulus)
        return jnp.cos(angle), jnp.sin(angle)

    facet_turns = jnp.bitwise_and(column * position, subgrids - 1)
    return {
        "start": parts(column * (position * (width // LANES) + lane), image_width // LANES),
        "cell": parts(column * lane, image_width),
        "tile": parts(column * lane, image_width // LANES),
        "inner": parts(column * (2 * lane + 1), 2 * image_width),
        "middle": parts(
            column * (width - 1) + 2 * width * facet_turns + 0 * lane, 2 * image_width
        ),
    }


def encode_kernel(
    slab_hbm, window_hbm, offsets_ref, coarse_hbm, fine_hbm, turn_hbm, flip_hbm, out_hbm, cells_hbm,
    slab_ref, window_ref, coarse_ref, fine_ref, turn_ref, flip_ref,
    phase_ref, side_ref, turn_table_ref, wave_ref, total_ref,
    out_ref, cells_ref, sems, out_sems,
):
    columns = slab_ref.shape[0] // 2
    width = slab_ref.shape[1]
    half = width // 2
    subgrids = offsets_ref.shape[1]
    rows = CONTRIB // FINE
    pairs = (
        (slab_hbm, slab_ref), (window_hbm, window_ref), (coarse_hbm, coarse_ref),
        (fine_hbm, fine_ref), (turn_hbm, turn_ref), (flip_hbm, flip_ref),
    )
    copies = [pltpu.make_async_copy(a, b, sems.at[n]) for n, (a, b) in enumerate(pairs)]
    for copy in copies:
        copy.start()
    turns = offset_tables(offsets_ref, lax.axis_index("facet"), width)
    (cos_a, sin_a), (cos_b, sin_b) = turns["start"], turns["cell"]
    for tile in range(width // LANES):
        c, s = cos_a[:, tile : tile + 1], sin_a[:, tile : tile + 1]
        span = slice(tile * LANES, (tile + 1) * LANES)
        cells_ref[0, :, span] = c * cos_b - s * sin_b
        cells_ref[1, :, span] = s * cos_b + c * sin_b
    leaving = [pltpu.make_async_copy(cells_ref, cells_hbm, out_sems.at[subgrids // SENT])]
    leaving[0].start()
    high, low, centre = turns["tile"], turns["inner"], turns["middle"]
    for tile in range(half // LANES):
        c, s = high[0][:, tile : tile + 1], high[1][:, tile : tile + 1]
        span = slice(tile * LANES, (tile + 1) * LANES)
        phase_ref[0, :, span] = c * low[0] - s * low[1]
        phase_ref[1, :, span] = s * low[0] + c * low[1]
    for copy in copies:
        copy.wait()

    def windowed(span):
        product = slab_ref[:, span].astype(jnp.float32) * window_ref[:, span]
        return product.astype(jnp.bfloat16)

    def stage_columns(tile, fine):
        span = slice(tile * STEP, (tile + 1) * STEP)
        slot = tile % 2
        if fine == 0:
            side_ref[0] = windowed(
                slice(half + tile * STEP, half + (tile + 1) * STEP)
            ).astype(jnp.float32)
            side_ref[1] = lax.dot_general(
                windowed(slice(half - (tile + 1) * STEP, half - tile * STEP)), flip_ref[...], NN,
                preferred_element_type=jnp.float32,
            )
        sides = []
        for n in range(2):
            re, im = side_ref[n, :columns], side_ref[n, columns:]
            if fine > 0:
                row = (2 * fine + n) * 2
                c, s = fine_ref[row : row + 1, span], fine_ref[row + 1 : row + 2, span]
                re, im = re * c + im * s, im * c - re * s
            sides.append((re, im))
        (re_p, im_p), (re_m, im_m) = sides
        upper = slice(2 * columns * fine, 2 * columns * fine + columns)
        lower = slice(2 * columns * fine + columns, 2 * columns * (fine + 1))
        wave_ref[slot, upper, :STEP] = (re_p + re_m).astype(jnp.bfloat16)
        wave_ref[slot, lower, :STEP] = (im_p + im_m).astype(jnp.bfloat16)
        wave_ref[slot, upper, STEP:] = (im_p - im_m).astype(jnp.bfloat16)
        wave_ref[slot, lower, STEP:] = (re_m - re_p).astype(jnp.bfloat16)

    def stage_rows(tile, s):
        span = slice(tile * STEP, (tile + 1) * STEP)
        where = slice(s * rows, (s + 1) * rows)
        cj, sj = coarse_ref[0, :, span], coarse_ref[1, :, span]
        co, so = phase_ref[0, s : s + 1, span], phase_ref[1, s : s + 1, span]
        turn_table_ref[tile % 2, where, :STEP] = (co * cj - so * sj).astype(jnp.bfloat16)
        turn_table_ref[tile % 2, where, STEP:] = (so * cj + co * sj).astype(jnp.bfloat16)

    cm, sm = turn_ref[0], turn_ref[1]
    scale = width ** (-0.5)
    sign = jnp.where(
        lax.broadcasted_iota(jnp.int32, (1, 2 * columns), 1) < columns, scale, -scale
    )

    def finish(s):
        co, so = centre[0][s : s + 1], centre[1][s : s + 1]
        c = (co * cm + so * sm) * scale
        d = (so * cm - co * sm) * sign
        blocks = []
        for fine in range(FINE):
            block = total_ref[s * rows : (s + 1) * rows, fine * LANES : (fine + 1) * LANES]
            blocks.append(block * c + pltpu.roll(block, columns, 1) * d)
        out_ref[s] = jnp.concatenate(blocks, 0).astype(jnp.bfloat16).T

    steps = half // STEP
    each = subgrids // BLOCKS
    for fine in range(FINE):
        stage_columns(0, fine)
    for s in range(subgrids):
        stage_rows(0, s)
    for tile in range(steps):
        for block in range(BLOCKS):
            where = slice(block * each * rows, (block + 1) * each * rows)
            part = lax.dot_general(
                turn_table_ref[tile % 2, where], wave_ref[tile % 2], NT,
                preferred_element_type=jnp.float32,
            )
            if tile == 0:
                total_ref[where] = part
            else:
                total_ref[where] += part
            if tile + 1 < steps:
                for fine in range(block * FINE // BLOCKS, (block + 1) * FINE // BLOCKS):
                    stage_columns(tile + 1, fine)
                for s in range(block * each, (block + 1) * each):
                    stage_rows(tile + 1, s)
            else:
                for s in range(block * each, (block + 1) * each):
                    finish(s)
                    if s % SENT == SENT - 1:
                        done = slice(s + 1 - SENT, s + 1)
                        copy = pltpu.make_async_copy(
                            out_ref.at[done], out_hbm.at[done], out_sems.at[s // SENT]
                        )
                        copy.start()
                        leaving.append(copy)
    for copy in leaving:
        copy.wait()


def grid_kernel(
    recv_ref, kernel_ref, cos_ref, sin_ref, counts_ref, part_ref, out_ref, re_ref, im_ref
):
    facets = recv_ref.shape[0]
    columns = recv_ref.shape[1] // 2
    cells = re_ref.shape[1]
    half = facets // 2
    re_ref[...] = jnp.zeros_like(re_ref)
    im_ref[...] = jnp.zeros_like(im_ref)

    for f in range(facets // 4):
        first, second, third, fourth = (
            recv_ref[n].astype(jnp.float32) for n in (f, f + half, facets - 1 - f, half - 1 - f)
        )
        for parity in range(2):
            span = slice(parity * cells // 2, (parity + 1) * cells // 2)
            near = first + second if parity == 0 else first - second
            far = third + fourth if parity == 0 else third - fourth
            both = jnp.concatenate([near + far, near - far], 0).astype(jnp.bfloat16)
            wide = lax.dot_general(
                both, kernel_ref[:, span], NN, preferred_element_type=jnp.float32
            )
            even_re, even_im = wide[:columns], wide[columns : 2 * columns]
            odd_re, odd_im = wide[2 * columns : 3 * columns], wide[3 * columns :]
            c, s = cos_ref[f : f + 1, span], sin_ref[f : f + 1, span]
            re_ref[:, span] += even_re * c + odd_im * s
            im_ref[:, span] += even_im * c - odd_re * s

    counts = lax.dot_general(
        counts_ref[...].astype(jnp.float32).astype(jnp.bfloat16), part_ref[...], NN,
        preferred_element_type=jnp.float32,
    )
    weights = jnp.where(counts > 0, 1.0 / jnp.maximum(counts, 1.0), 0.0) * (
        (2 * facets) ** (-0.5)
    )
    re = re_ref[...] * weights
    im = im_ref[...] * weights
    per = out_ref.shape[1] // 2
    for layer in range(out_ref.shape[0]):
        span = slice(layer * per, (layer + 1) * per)
        out_ref[layer] = jnp.concatenate([re[span], im[span]], 0).astype(jnp.bfloat16)


def back_kernel(recv_ref, kernel_ref, cos_ref, sin_ref, out_ref, rows_ref):
    layers = recv_ref.shape[0]
    facets = out_ref.shape[0]
    total = recv_ref[0].astype(jnp.float32)
    for layer in range(1, layers):
        total = total + recv_ref[layer].astype(jnp.float32)
    per = total.shape[0] // 2
    re, im = total[:per], total[per:]
    for f in range(facets):
        c = cos_ref[f : f + 1, :]
        s = sin_ref[f : f + 1, :]
        turned = jnp.concatenate([re * c - im * s, im * c + re * s], 0)
        rows_ref[f * 2 * per : (f + 1) * 2 * per, :] = turned.astype(jnp.bfloat16)
    back = lax.dot_general(
        rows_ref[...], kernel_ref[...], NT, preferred_element_type=jnp.float32
    )
    out_ref[...] = (back * 0.5).astype(jnp.bfloat16).reshape(out_ref.shape)


def decode_kernel(
    recv_ref, window_ref, phases_ref, table_ref, out_ref
):
    subgrids = recv_ref.shape[0]
    per = recv_ref.shape[1] // 2
    width = out_ref.shape[2]
    rows = recv_ref[...].astype(jnp.float32)
    re, im = rows[:, :per], rows[:, per:]
    left_re = jnp.concatenate([re, im], 2).reshape(subgrids * per, 2 * CONTRIB).astype(jnp.bfloat16)
    left_im = jnp.concatenate([im, -re], 2).reshape(subgrids * per, 2 * CONTRIB).astype(jnp.bfloat16)
    scale = (subgrids * CONTRIB) ** (-0.5)
    for tile in range(width // 256):
        span = slice(tile * 256, (tile + 1) * 256)
        table = table_ref[:, span]
        zr = lax.dot_general(left_re, table, NN, preferred_element_type=jnp.float32)
        zi = lax.dot_general(left_im, table, NN, preferred_element_type=jnp.float32)
        out_re, out_im = None, None
        for s in range(subgrids):
            a = zr[s * per : (s + 1) * per]
            b = zi[s * per : (s + 1) * per]
            pr = phases_ref[0, s : s + 1, span]
            pi = phases_ref[1, s : s + 1, span]
            re_term = pr * a - pi * b
            im_term = pr * b + pi * a
            out_re = re_term if out_re is None else out_re + re_term
            out_im = im_term if out_im is None else out_im + im_term
        taper = window_ref[:, span] * scale
        out_ref[0, :, span] = out_re * taper
        out_ref[1, :, span] = out_im * taper


def params(mebibytes):
    return pltpu.CompilerParams(vmem_limit_bytes=mebibytes * 2**20)


def shards(slabs, window, density, offsets):
    layers = lax.axis_size("layer")
    facets = lax.axis_size("facet")
    columns, width = slabs.shape[2], slabs.shape[3]
    per = columns // layers
    sample_step = SUB // CONTRIB
    image_width = width * facets
    table = jnp.asarray(step_table(width, image_width, sample_step))
    folds = [jnp.asarray(part) for part in fold_tables(width, image_width, sample_step)]
    cells = np.concatenate([np.arange(0, SUB, 2), np.arange(1, SUB, 2)])
    spreading = np.ascontiguousarray(kernel_table(sample_step)[:, cells])
    parting = np.eye(SUB)[:, cells].astype(ml_dtypes.bfloat16)
    spread = jnp.asarray(spreading)
    order = np.arange(CONTRIB).reshape(CONTRIB // FINE, FINE).T.reshape(-1)
    spread_in = jnp.asarray(np.ascontiguousarray(spreading[order]))
    cos_u, sin_u = (
        jnp.asarray(np.ascontiguousarray(part[:, cells])) for part in centre_phases(facets)
    )

    window_row = window.reshape(1, width)

    whole = pl.BlockSpec(memory_space=pltpu.VMEM)
    anywhere = pl.BlockSpec(memory_space=pl.ANY)
    rows = facets * CONTRIB // FINE
    wide = 2 * columns * FINE
    half = width // 2
    outgoing, cell_phases = pl.pallas_call(
        encode_kernel,
        out_shape=(
            jax.ShapeDtypeStruct((facets, 2 * columns, CONTRIB), jnp.bfloat16),
            jax.ShapeDtypeStruct((2, facets, width), jnp.float32),
        ),
        in_specs=[anywhere, anywhere, whole] + [anywhere] * 4,
        out_specs=(anywhere, anywhere),
        scratch_shapes=[
            pltpu.VMEM((2 * columns, width), jnp.bfloat16),
            pltpu.VMEM((1, width), jnp.float32),
            pltpu.VMEM((2, CONTRIB // FINE, half), jnp.float32),
            pltpu.VMEM((4 * FINE, half), jnp.float32),
            pltpu.VMEM((2, CONTRIB // FINE, LANES), jnp.float32),
            pltpu.VMEM((STEP, STEP), jnp.bfloat16),
            pltpu.VMEM((2, facets, half), jnp.float32),
            pltpu.VMEM((2, 2 * columns, STEP), jnp.float32),
            pltpu.VMEM((2, rows, 2 * STEP), jnp.bfloat16),
            pltpu.VMEM((2, wide, 2 * STEP), jnp.bfloat16),
            pltpu.VMEM((rows, wide), jnp.float32),
            pltpu.VMEM((facets, 2 * columns, CONTRIB), jnp.bfloat16),
            pltpu.VMEM((2, facets, width), jnp.float32),
            pltpu.SemaphoreType.DMA((6,)),
            pltpu.SemaphoreType.DMA((facets // SENT + 1,)),
        ],
        compiler_params=params(60),
        name="encode",
    )(slabs.reshape(2 * columns, width), window_row, offsets.reshape(1, facets), *folds)

    received = lax.all_to_all(outgoing, "facet", split_axis=0, concat_axis=0, tiled=True)

    gridded = pl.pallas_call(
        grid_kernel,
        out_shape=jax.ShapeDtypeStruct((layers, 2 * per, SUB), jnp.bfloat16),
        in_specs=[whole] * 6,
        out_specs=whole,
        scratch_shapes=[pltpu.VMEM((columns, SUB), jnp.float32)] * 2,
        compiler_params=params(60),
        name="subgrid",
    )(received, spread_in, cos_u, sin_u, density[0], jnp.asarray(parting))

    by_layer = lax.all_to_all(gridded, "layer", split_axis=0, concat_axis=0, tiled=True)

    back_out = pl.pallas_call(
        back_kernel,
        out_shape=jax.ShapeDtypeStruct((facets, 2 * per, CONTRIB), jnp.bfloat16),
        in_specs=[whole] * 4,
        out_specs=whole,
        scratch_shapes=[pltpu.VMEM((facets * 2 * per, SUB), jnp.bfloat16)],
        compiler_params=params(60),
        name="back",
    )(by_layer, spread, cos_u, sin_u)

    returned = lax.all_to_all(back_out, "facet", split_axis=0, concat_axis=0, tiled=True)

    return pl.pallas_call(
        decode_kernel,
        out_shape=jax.ShapeDtypeStruct((2, per, width), jnp.float32),
        in_specs=[whole] * 4,
        out_specs=whole,
        compiler_params=params(60),
        name="decode",
    )(returned, window_row, cell_phases, table)


def solution(mesh):
    placed = (P("layer", None, None, "facet"), P("facet"), P("layer", None, "facet"), P())
    return jax.shard_map(
        shards, mesh=mesh, in_specs=placed, out_specs=P(None, "layer", "facet"), check_vma=False
    )
```
